32 devices in a mesh: row: 4 (over x, core), col: 8 (over z, y).
Axes of the slice: x: 2, y: 2, z: 4, core: 2. Of those that a mesh axis runs over, the one named last changes fastest.
Arguments:
- kernel: float32 [16384, 16384], P('row', 'col'), may hold values from 0 to 20, as said below
Outputs:
- factored: float32 [16384, 16384], P('row', 'col')
The draws below stay inside these ranges and needn't reach their ends.
Inputs may be any that keep to these rules, and one draw needn't show every extreme that they name: `kernel`: in logical order K is symmetric and positive definite.
All inputs are finite; a program needn't handle non-finite values.
Results may differ from the reference program's by a relative error of at most 0.0003.
Values sent between devices are 32-bit elements; how exact they have to be, the bound alone decides.
No kernel may reach another device: no remote copies, remote signals or barrier semaphores. Data moves between devices by JAX's collectives and lax.ppermute only.
A program may use at most 192 MiB of HBM per device.

```python
import jax
import jax.numpy as jnp
from jax import lax

NB = 512
ORDER = 16384
STEPS = 1
N_ROW = 4
N_COL = 8


def draw_kernel(key, part):
    first_key, second_key = jax.random.split(key, 2)
    features = jax.random.normal(first_key, (ORDER, 16), jnp.float32)
    squares = jnp.sum(features * features, axis=1)
    inner = jnp.dot(features, features.T, precision=lax.Precision.HIGHEST)
    distance = jnp.maximum(squares[:, None] + squares[None, :] - 2.0 * inner, 0.0)
    gram = jnp.exp(distance * (-1.0 / 16.0))
    gram = 0.5 * (gram + gram.T)
    positions = jnp.arange(ORDER)
    on_diagonal = positions[:, None] == positions[None, :]
    ridge = jax.random.uniform(second_key, (ORDER,), jnp.float32, 0.05, 0.1)
    logical = jnp.where(on_diagonal, 1.0 + ridge[:, None], gram)
    block_rows = ORDER // (NB * N_ROW)
    block_cols = ORDER // (NB * N_COL)
    shaped = logical.reshape(block_rows, N_ROW, NB, block_cols, N_COL, NB)
    return shaped.transpose(1, 0, 2, 4, 3, 5).reshape(ORDER, ORDER)


def setup_inputs(seed: int = 0) -> dict:
    keys = jax.random.split(jax.random.key(seed), 2)
    return {
        "kernel": draw_kernel(jax.random.fold_in(keys[1], 71), 0),
    }


def to_logical(stored):
    block_rows = ORDER // (NB * N_ROW)
    block_cols = ORDER // (NB * N_COL)
    shaped = stored.reshape(N_ROW, block_rows, NB, N_COL, block_cols, NB)
    return shaped.transpose(1, 0, 2, 4, 3, 5).reshape(ORDER, ORDER)

def to_storage(logical):
    block_rows = ORDER // (NB * N_ROW)
    block_cols = ORDER // (NB * N_COL)
    shaped = logical.reshape(block_rows, N_ROW, NB, block_cols, N_COL, NB)
    return shaped.transpose(1, 0, 2, 4, 3, 5).reshape(ORDER, ORDER)

def reference(kernel):
    matrix = to_logical(kernel)
    for section_index in range(STEPS):
        lower_edge = section_index * NB
        upper_edge = lower_edge + NB
        factor = jnp.linalg.cholesky(matrix[lower_edge:upper_edge, lower_edge:upper_edge])
        below = matrix[upper_edge:, lower_edge:upper_edge]
        solved = jax.scipy.linalg.solve_triangular(factor, below.T, lower=True).T
        update = lax.dot_general(solved, solved, (((1,), (1,)), ((), ())), precision=lax.Precision.HIGHEST)
        matrix = matrix.at[upper_edge:, upper_edge:].set(matrix[upper_edge:, upper_edge:] - update)
        matrix = matrix.at[lower_edge:upper_edge, lower_edge:upper_edge].set(factor)
        matrix = matrix.at[upper_edge:, lower_edge:upper_edge].set(solved)
        matrix = matrix.at[lower_edge:upper_edge, upper_edge:].set(jnp.zeros_like(matrix[lower_edge:upper_edge, upper_edge:]))
    return to_storage(matrix)
```

```python
import functools

import jax
import jax.numpy as jnp
from jax import lax
from jax.experimental import pallas as pl
from jax.experimental.pallas import tpu as pltpu
from jax.sharding import PartitionSpec as P

NB = 512
SUB = 128
LANES = 8
VMEM_BYTES = 60 * 1024 * 1024
LOWER = [(i, j) for i in range(NB // SUB) for j in range(i + 1)]
EXACT = lax.Precision.HIGHEST


def dot_nt(a, b):
    return lax.dot_general(
        a, b, (((1,), (1,)), ((), ())), precision=EXACT, preferred_element_type=jnp.float32
    )


def dot_nn(a, b):
    return lax.dot_general(
        a, b, (((1,), (0,)), ((), ())), precision=EXACT, preferred_element_type=jnp.float32
    )


def split(value):
    high = value.astype(jnp.bfloat16)
    low = (value - high.astype(jnp.float32)).astype(jnp.bfloat16)
    return high, low


def small_cholesky(block):
    groups = SUB // LANES
    lane = lax.broadcasted_iota(jnp.int32, (LANES, SUB), 1)
    sub = lax.broadcasted_iota(jnp.int32, (LANES, SUB), 0)
    left = [block[g * LANES : (g + 1) * LANES] for g in range(groups)]
    right = [jnp.where(lane == sub + g * LANES, 1.0, 0.0) for g in range(groups)]
    for i in range(0, SUB, 2):
        g0, o = divmod(i, LANES)
        head = left[g0]
        row0, row1 = head[o : o + 1], head[o + 1 : o + 2]
        side0, side1 = right[g0][o : o + 1], right[g0][o + 1 : o + 2]
        inv0 = 1.0 / row0[:, i : i + 1]
        ratio = row0[:, i + 1 : i + 2] * inv0
        pivot1 = row1[:, i + 1 : i + 2] - row0[:, i + 1 : i + 2] * ratio
        inv1 = 1.0 / pivot1
        row1 = row1 - ratio * row0
        side1 = side1 - ratio * side0
        row0s, side0s = row0 * inv0, side0 * inv0
        row1s, side1s = row1 * inv1, side1 * inv1
        for g in range(g0, groups):
            col0 = left[g][:, i : i + 1]
            col1 = left[g][:, i + 1 : i + 2] - col0 * ratio
            if g == g0:
                if o + 2 < LANES:
                    below = sub > o + 1
                    new_left = left[g] - jnp.where(below, col0, 0.0) * row0s - jnp.where(below, col1, 0.0) * row1s
                    new_right = right[g] - jnp.where(below, col0, 0.0) * side0s - jnp.where(below, col1, 0.0) * side1s
                else:
                    new_left, new_right = left[g], right[g]
                left[g] = jnp.where(sub == o + 1, row1, new_left)
                right[g] = jnp.where(sub == o + 1, side1, new_right)
            else:
                left[g] = left[g] - col0 * row0s - col1 * row1s
                right[g] = right[g] - col0 * side0s - col1 * side1s
    upper, inverse = [], []
    for g in range(groups):
        row = sub + g * LANES
        pivot = jnp.sum(jnp.where(lane == row, left[g], 0.0), axis=1, keepdims=True)
        scale = lax.rsqrt(pivot)
        upper.append(jnp.where(lane >= row, left[g] * scale, 0.0))
        inverse.append(jnp.where(lane <= row, right[g] * scale, 0.0))
    return jnp.concatenate(upper, 0), jnp.concatenate(inverse, 0)


def factor_kernel(first_ref, second_ref, factor_ref, inv_ref, inv_t_ref, work):
    half = first_ref.shape[0]
    count = NB // SUB
    factor_ref[...] = jnp.zeros_like(factor_ref)
    inv_ref[...] = jnp.zeros_like(inv_ref)
    inv_t_ref[...] = jnp.zeros_like(inv_t_ref)
    for n, (i, j) in enumerate(LOWER):
        value = first_ref[n] if n < half else second_ref[n - half]
        work[i * SUB : (i + 1) * SUB, j * SUB : (j + 1) * SUB] = value
    for k in range(count):
        a, b = k * SUB, (k + 1) * SUB
        upper, inverse = small_cholesky(work[a:b, a:b])
        factor_ref[a:b, a:b] = upper.T
        inverse_t = inverse.T
        inv_ref[a:b, a:b] = inverse
        inv_t_ref[a:b, a:b] = inverse_t
        if k + 1 < count:
            panel = dot_nn(work[b:, a:b], inverse_t)
            factor_ref[b:, a:b] = panel
            for j in range(k + 1, count):
                c, d = j * SUB, (j + 1) * SUB
                work[c:, c:d] -= dot_nt(panel[c - b :], panel[c - b : d - b])
        if k:
            partial = dot_nt(inv_t_ref[:a, :a], factor_ref[a:b, :a])
            part = -dot_nn(partial, inverse_t)
            inv_t_ref[:a, a:b] = part
            inv_ref[a:b, :a] = part.T


def factorize(first, second):
    square = jax.ShapeDtypeStruct((NB, NB), jnp.float32)
    return pl.pallas_call(
        factor_kernel,
        out_shape=(square, square, square),
        in_specs=[pl.BlockSpec(memory_space=pltpu.VMEM)] * 2,
        out_specs=(pl.BlockSpec(memory_space=pltpu.VMEM),) * 3,
        scratch_shapes=[pltpu.VMEM((NB, NB), jnp.float32)],
        compiler_params=pltpu.CompilerParams(vmem_limit_bytes=VMEM_BYTES),
        cost_estimate=pl.CostEstimate(flops=2 * NB**3, bytes_accessed=6 * NB * NB * 4, transcendentals=0),
        name="factor_corner",
    )(first, second)


def across_kernel(inv_ref, rows_ref, out_ref):
    value = dot_nn(inv_ref[...], rows_ref[...])
    high, low = split(value)
    out_ref[:NB] = high
    out_ref[NB : 2 * NB] = high
    out_ref[2 * NB :] = low


def solve_across(inv, rows):
    width = rows.shape[1]
    return pl.pallas_call(
        across_kernel,
        grid=(width // NB,),
        out_shape=jax.ShapeDtypeStruct((3 * NB, width), jnp.bfloat16),
        in_specs=[
            pl.BlockSpec((NB, NB), lambda i: (0, 0)),
            pl.BlockSpec((NB, NB), lambda i: (0, i)),
        ],
        out_specs=pl.BlockSpec((3 * NB, NB), lambda i: (0, i)),
        compiler_params=pltpu.CompilerParams(vmem_limit_bytes=VMEM_BYTES),
        cost_estimate=pl.CostEstimate(
            flops=2 * NB * NB * width, bytes_accessed=10 * NB * width, transcendentals=0
        ),
        name="solve_across",
    )(inv, rows)


def update_kernel(count, tile, info, *refs):
    chunks = refs[:count]
    inv_t_ref, factor_ref, across_ref, matrix_ref = refs[count : count + 4]
    out_ref, panel, panel3 = refs[-3:]
    i, j = pl.program_id(0), pl.program_id(1)
    first_row = jnp.logical_and(info[count] == 0, info[i] == 0)
    first_col = jnp.logical_and(info[count + 1] == 0, j == 0)

    @pl.when(j == 0)
    def _():
        for n in range(count):

            @pl.when(i == n)
            def _():
                panel[...] = dot_nn(chunks[n][...], inv_t_ref[...])

        high, low = split(panel[...])
        panel3[:, :NB] = high
        panel3[:, NB : 2 * NB] = low
        panel3[:, 2 * NB :] = high

        @pl.when(first_row)
        def _():
            panel[...] = factor_ref[...]

    @pl.when(first_row)
    def _():
        out_ref[...] = jnp.zeros_like(out_ref)

    @pl.when(jnp.logical_not(first_row))
    def _():
        columns = pl.ds(pl.multiple_of(j * tile, tile), tile)
        product = jnp.dot(panel3[...], across_ref[:, columns], preferred_element_type=jnp.float32)
        out_ref[...] = matrix_ref[...] - product

    @pl.when(first_col)
    def _():
        out_ref[:, :NB] = panel[...]


def update(info, chunks, inv_t, factor, across, matrix, base):
    count = len(chunks)
    rows, width = matrix.shape
    tile = 2 * NB if width % (2 * NB) == 0 else NB
    whole = lambda i, j, info: (0, 0)
    moving = lambda i, j, info: (info[i], j)
    square = pl.BlockSpec((NB, NB), whole)
    in_specs = [square] * (count + 2) + [
        pl.BlockSpec((3 * NB, width), whole),
        pl.BlockSpec((NB, tile), moving),
    ]
    operands = [info, *chunks, inv_t, factor, across, matrix]
    aliases = {}
    if base is not None:
        in_specs.append(pl.BlockSpec(memory_space=pl.ANY))
        operands.append(base)
        aliases = {len(operands) - 1: 0}
    return pl.pallas_call(
        functools.partial(update_kernel, count, tile),
        grid_spec=pltpu.PrefetchScalarGridSpec(
            num_scalar_prefetch=1,
            grid=(count, width // tile),
            in_specs=in_specs,
            out_specs=pl.BlockSpec((NB, tile), moving),
            scratch_shapes=[
                pltpu.VMEM((NB, NB), jnp.float32),
                pltpu.VMEM((NB, 3 * NB), jnp.bfloat16),
            ],
        ),
        out_shape=jax.ShapeDtypeStruct(matrix.shape, jnp.float32),
        input_output_aliases=aliases,
        compiler_params=pltpu.CompilerParams(vmem_limit_bytes=VMEM_BYTES),
        cost_estimate=pl.CostEstimate(
            flops=6 * count * NB * NB * (width + 2 * NB),
            bytes_accessed=8 * count * NB * width,
            transcendentals=0,
        ),
        name="update_rows",
    )(*operands)


def spread(value, axes, index, order):
    reached = [0]
    for bit in order:
        pairs = [(n, n | bit) for n in reached]
        came = lax.ppermute(value, axes, pairs)
        done = sum(order[: order.index(bit)])
        value = jnp.where((index & ~done) == bit, came, value)
        reached = reached + [n | bit for n in reached]
    return value


def bits_of(size):
    return [1 << n for n in range(size.bit_length() - 1)]


def spread_corner(matrix, p, q, rows_axis, cols_axis):
    corner = matrix[:NB, :NB]
    pieces = jnp.stack(
        [corner[i * SUB : (i + 1) * SUB, j * SUB : (j + 1) * SUB] for i, j in LOWER]
    )
    half = len(LOWER) // 2
    low_bits = bits_of(cols_axis)
    high_bits = [cols_axis * b for b in bits_of(rows_axis)]
    core, across = high_bits[:1], high_bits[1:]
    one = across[::-1] + low_bits[:1] + low_bits[:0:-1] + core
    two = low_bits[:0:-1] + low_bits[:1] + across[::-1] + core
    index = p * cols_axis + q
    axes = ("row", "col")
    return (
        spread(pieces[:half], axes, index, one),
        spread(pieces[half:], axes, index, two),
    )


def ring_positions(cols_axis):
    half = cols_axis // 2
    return [2 * n for n in range(half)] + [2 * n + 1 for n in reversed(range(half))]


def gather_rows(matrix, p, q, rows_axis, cols_axis):
    groups = cols_axis // rows_axis
    came = None
    for t in range(rows_axis):
        block = matrix[:NB, t * NB : (t + 1) * NB].T
        pairs = []
        for r in range(cols_axis):
            h, target = divmod(r, rows_axis)
            pairs.append((r, target * cols_axis + h * rows_axis + (target ^ t)))
        piece = lax.ppermute(block, ("row", "col"), pairs)
        came = piece if came is None else came + piece
    ring = ring_positions(cols_axis)
    table = jnp.array(ring, jnp.int32)
    position = jnp.array([ring.index(n) for n in range(cols_axis)], jnp.int32)[q]

    def slot(shift):
        source = table[(position + shift) % cols_axis]
        h = source // rows_axis
        return groups * ((source % rows_axis) ^ p) + h

    up = [(ring[n], ring[(n + 1) % cols_axis]) for n in range(cols_axis)]
    down = [(b, a) for a, b in up]
    found = [(slot(0), came)]
    going, coming = came, came
    for step in range(1, cols_axis // 2):
        going = lax.ppermute(going, "col", up)
        coming = lax.ppermute(coming, "col", down)
        found.append((slot(-step), going))
        found.append((slot(step), coming))
    top = lax.ppermute(going[: NB // 2], "col", up)
    bottom = lax.ppermute(coming[NB // 2 :], "col", down)
    found.append((slot(cols_axis // 2), jnp.concatenate([top, bottom], 0)))
    return found


def from_root(value, axis, source):
    kept = jnp.where(lax.axis_index(axis) == source, value, 0).astype(value.dtype)
    return lax.psum(kept, axis)


def on_device(matrix):
    rows_axis = lax.axis_size("row")
    cols_axis = lax.axis_size("col")
    p, q = lax.axis_index("row"), lax.axis_index("col")
    row_blocks = matrix.shape[0] // NB
    col_blocks = matrix.shape[1] // NB
    first, second = spread_corner(matrix, p, q, rows_axis, cols_axis)
    if row_blocks == cols_axis and col_blocks == rows_axis:
        found = gather_rows(matrix, p, q, rows_axis, cols_axis)
    else:
        column = from_root(matrix[:, :NB], "col", 0)
        found = [(jnp.int32(s), column[s * NB : (s + 1) * NB]) for s in range(row_blocks)]
    above = spread(matrix[:NB], "row", p, bits_of(rows_axis)[::-1])
    factor, inv, inv_t = factorize(first, second)
    across = solve_across(inv, above)
    early = max(1, len(found) - 3)
    out = None
    for part in (found[:early], found[early:]):
        if part:
            info = jnp.stack([s for s, _ in part] + [p, q]).astype(jnp.int32)
            out = update(info, [c for _, c in part], inv_t, factor, across, matrix, out)
    return out


def solution(mesh):
    in_specs = (P("row", "col"),)
    out_specs = P("row", "col")
    return jax.shard_map(
        on_device, mesh=mesh, in_specs=in_specs, out_specs=out_specs, check_vma=False
    )
```

```python
import functools

import jax
import jax.numpy as jnp
import numpy as np
from jax import lax
from jax.experimental import pallas as pl
from jax.experimental.pallas import tpu as pltpu
from jax.sharding import PartitionSpec as P

NB = 512
SUB = 128
LANES = 8
COUNT = NB // SUB
VMEM_BYTES = 60 * 1024 * 1024
LOWER = [(i, j) for i in range(COUNT) for j in range(i + 1)]
HALF = len(LOWER) // 2
EXACT = lax.Precision.HIGHEST
PARAMS = pltpu.CompilerParams(vmem_limit_bytes=VMEM_BYTES)
SQUARE = jax.ShapeDtypeStruct((NB, NB), jnp.float32)
IN_VMEM = pl.BlockSpec(memory_space=pltpu.VMEM)
ANYWHERE = pl.BlockSpec(memory_space=pl.ANY)


def dot_nt(a, b):
    return lax.dot_general(
        a, b, (((1,), (1,)), ((), ())), precision=EXACT, preferred_element_type=jnp.float32
    )


def dot_nn(a, b):
    return lax.dot_general(
        a, b, (((1,), (0,)), ((), ())), precision=EXACT, preferred_element_type=jnp.float32
    )


def split2(value):
    high = value.astype(jnp.bfloat16)
    low = (value - high.astype(jnp.float32)).astype(jnp.bfloat16)
    return high, low


def split3(value):
    high = value.astype(jnp.bfloat16)
    rest = value - high.astype(jnp.float32)
    middle, low = split2(rest)
    return high, middle, low


def store_parts(ref, value, axis, pattern):
    parts = split3(value)
    for n, k in enumerate(pattern):
        place = slice(n * NB, (n + 1) * NB)
        if axis:
            ref[:, place] = parts[k]
        else:
            ref[place] = parts[k]


LEFT_PARTS = (0, 1, 2, 0, 1, 0)
RIGHT_PARTS = (0, 0, 0, 1, 1, 2)


def pack_kernel(matrix_ref, first_ref, second_ref):
    for n, (i, j) in enumerate(LOWER):
        target, place = (first_ref, n) if n < HALF else (second_ref, n - HALF)
        target[place] = matrix_ref[i * SUB : (i + 1) * SUB, j * SUB : (j + 1) * SUB]


def pack_corner(matrix):
    part = jax.ShapeDtypeStruct((HALF, SUB, SUB), jnp.float32)
    whole = pl.BlockSpec((HALF, SUB, SUB), lambda i: (0, 0, 0))
    return pl.pallas_call(
        pack_kernel,
        grid=(1,),
        out_shape=(part, part),
        in_specs=[pl.BlockSpec((NB, NB), lambda i: (0, 0))],
        out_specs=(whole, whole),
        compiler_params=PARAMS,
        name="pack_corner",
    )(matrix)


def turn_kernel(count, matrix_ref, *refs):
    for t in range(count):
        refs[t][...] = matrix_ref[:, t * NB : (t + 1) * NB].T


def turn_blocks(matrix, count):
    square = pl.BlockSpec((NB, NB), lambda i: (0, 0))
    return pl.pallas_call(
        functools.partial(turn_kernel, count),
        grid=(1,),
        out_shape=(SQUARE,) * count,
        in_specs=[pl.BlockSpec((NB, count * NB), lambda i: (0, 0))],
        out_specs=(square,) * count,
        compiler_params=PARAMS,
        name="turn_blocks",
    )(matrix)


def reciprocal(value):
    guess = pl.reciprocal(value, approx=True)
    guess = guess * (2.0 - value * guess)
    return guess * (2.0 - value * guess)


def small_cholesky(block):
    groups = SUB // LANES
    shape = (LANES, SUB)
    lane = lax.broadcasted_iota(jnp.int32, shape, 1)
    sub = lax.broadcasted_iota(jnp.int32, shape, 0)
    left = [block[g * LANES : (g + 1) * LANES] for g in range(groups)]
    right = [jnp.where(lane == sub + g * LANES, 1.0, 0.0) for g in range(groups)]
    for g0 in range(groups):
        i = g0 * LANES
        head, side = left[g0], right[g0]
        columns = [jnp.broadcast_to(head[:, i + j : i + j + 1], shape) for j in range(LANES)]
        ratios, heads, sides = [], [], []
        for k in range(LANES):
            inverse = reciprocal(columns[k][k : k + 1])
            ratio = {j: columns[j][k : k + 1] * inverse for j in range(k + 1, LANES)}
            scaled_head = head[k : k + 1] * inverse
            scaled_side = side[k : k + 1] * inverse
            ratios.append(ratio)
            heads.append(scaled_head)
            sides.append(scaled_side)
            if k + 1 < LANES:
                below = jnp.where(sub > k, columns[k], 0.0)
                for j in range(k + 1, LANES):
                    columns[j] = columns[j] - below * ratio[j]
                head = head - below * scaled_head
                side = side - below * scaled_side
        left[g0], right[g0] = head, side
        for g in range(g0 + 1, groups):
            own = [jnp.broadcast_to(left[g][:, i + j : i + j + 1], shape) for j in range(LANES)]
            body, tail = left[g], right[g]
            for k in range(LANES):
                for j in range(k + 1, LANES):
                    own[j] = own[j] - own[k] * ratios[k][j]
                body = body - own[k] * heads[k]
                tail = tail - own[k] * sides[k]
            left[g], right[g] = body, tail
    upper, inverse = [], []
    for g in range(groups):
        row = sub + g * LANES
        pivot = jnp.sum(jnp.where(lane == row, left[g], 0.0), axis=1, keepdims=True)
        scale = lax.rsqrt(pivot)
        upper.append(jnp.where(lane >= row, left[g] * scale, 0.0))
        inverse.append(jnp.where(lane <= row, right[g] * scale, 0.0))
    return jnp.concatenate(upper, 0), jnp.concatenate(inverse, 0)


def factor_block(k, work, inv_t):
    start = pl.multiple_of(k * SUB, SUB)
    here = pl.ds(start, SUB)
    upper, inverse = small_cholesky(work[here, here])
    inverse_t = inverse.T
    row = lax.broadcasted_iota(jnp.int32, (NB, SUB), 0)
    panel = jnp.where(row >= start + SUB, dot_nn(work[:, here], inverse_t), 0.0)
    work[...] -= dot_nt(panel, panel)
    work[:, here] = panel
    work[here, here] = upper.T
    column = lax.broadcasted_iota(jnp.int32, (SUB, NB), 1)
    before = jnp.where(column < start, work[here, :], 0.0)
    inv_t[:, here] = -dot_nn(dot_nt(inv_t[...], before), inverse_t)
    inv_t[here, here] = inverse_t


def factor_first_kernel(last, first_ref, second_ref, work, inv_t):
    inv_t[...] = jnp.zeros_like(inv_t)
    work[...] = jnp.zeros_like(work)
    for n, (i, j) in enumerate(LOWER):
        value = first_ref[n] if n < HALF else second_ref[n - HALF]
        work[i * SUB : (i + 1) * SUB, j * SUB : (j + 1) * SUB] = value

    @pl.loop(0, last)
    def _(k):
        factor_block(k, work, inv_t)


def factor_last_kernel(begin, work_in, inv_t_in, factor_ref, inv_ref, inv_t_ref):
    factor_ref[...] = work_in[...]
    inv_t_ref[...] = inv_t_in[...]

    @pl.loop(begin, COUNT)
    def _(k):
        factor_block(k, factor_ref, inv_t_ref)

    inv_ref[...] = inv_t_ref[...].T


FACTOR_COST = pl.CostEstimate(flops=2 * NB**3, bytes_accessed=4 * NB * NB * 4, transcendentals=0)


def factor_first(first, second):
    return pl.pallas_call(
        functools.partial(factor_first_kernel, COUNT // 2),
        out_shape=(SQUARE, SQUARE),
        in_specs=[IN_VMEM] * 2,
        out_specs=(IN_VMEM,) * 2,
        compiler_params=PARAMS,
        cost_estimate=FACTOR_COST,
        name="factor_first",
    )(first, second)


def factor_last(work, inv_t):
    return pl.pallas_call(
        functools.partial(factor_last_kernel, COUNT // 2),
        out_shape=(SQUARE, SQUARE, SQUARE),
        in_specs=[IN_VMEM] * 2,
        out_specs=(IN_VMEM,) * 3,
        compiler_params=PARAMS,
        cost_estimate=FACTOR_COST,
        name="factor_last",
    )(work, inv_t)


def across_kernel(count, info, inv_ref, *refs):
    sources, out_ref, left, right, rows, sem = refs[:count], *refs[count:]
    i = pl.program_id(0)

    @pl.when(i == 0)
    def _():
        for n in range(count):

            @pl.when(info[0] == n)
            def _():
                copy = pltpu.make_async_copy(sources[n].at[pl.ds(0, NB)], rows, sem)
                copy.start()
                copy.wait()

        store_parts(left, inv_ref[...], 1, LEFT_PARTS)

    columns = pl.ds(pl.multiple_of(i * NB, NB), NB)
    store_parts(right, rows[:, columns], 0, RIGHT_PARTS)
    value = jnp.dot(left[...], right[...], preferred_element_type=jnp.float32)
    high, low = split2(value)
    out_ref[:NB] = high
    out_ref[NB : 2 * NB] = high
    out_ref[2 * NB :] = low


def solve_across(info, inv, sources):
    width = sources[0].shape[1]
    count = len(sources)
    return pl.pallas_call(
        functools.partial(across_kernel, count),
        grid_spec=pltpu.PrefetchScalarGridSpec(
            num_scalar_prefetch=1,
            grid=(width // NB,),
            in_specs=[pl.BlockSpec((NB, NB), lambda i, info: (0, 0))] + [ANYWHERE] * count,
            out_specs=pl.BlockSpec((3 * NB, NB), lambda i, info: (0, i)),
            scratch_shapes=[
                pltpu.VMEM((NB, 6 * NB), jnp.bfloat16),
                pltpu.VMEM((6 * NB, NB), jnp.bfloat16),
                pltpu.VMEM((NB, width), jnp.float32),
                pltpu.SemaphoreType.DMA,
            ],
        ),
        out_shape=jax.ShapeDtypeStruct((3 * NB, width), jnp.bfloat16),
        compiler_params=PARAMS,
        cost_estimate=pl.CostEstimate(
            flops=12 * NB * NB * width, bytes_accessed=10 * NB * width, transcendentals=0
        ),
        name="solve_across",
    )(info, inv, *sources)


def update_kernel(count, tile, info, *refs):
    chunks = refs[:count]
    inv_t_ref, factor_ref, across_ref, matrix_ref = refs[count : count + 4]
    out_ref, panel, panel3, left, right = refs[-5:]
    i, j = pl.program_id(0), pl.program_id(1)
    first_row = jnp.logical_and(info[0] == 0, info[2 + i] == 0)
    first_col = jnp.logical_and(info[1] == 0, j == 0)

    @pl.when(jnp.logical_and(i == 0, j == 0))
    def _():
        store_parts(right, inv_t_ref[...], 0, RIGHT_PARTS)

    @pl.when(j == 0)
    def _():
        for n in range(count):

            @pl.when(i == n)
            def _():
                store_parts(left, chunks[n][...], 1, LEFT_PARTS)

        value = jnp.dot(left[...], right[...], preferred_element_type=jnp.float32)
        panel[...] = value
        high, low = split2(value)
        panel3[:, :NB] = high
        panel3[:, NB : 2 * NB] = low
        panel3[:, 2 * NB :] = high

        @pl.when(first_row)
        def _():
            panel[...] = factor_ref[...]

    @pl.when(first_row)
    def _():
        out_ref[...] = jnp.zeros_like(out_ref)

    @pl.when(jnp.logical_not(first_row))
    def _():
        columns = pl.ds(pl.multiple_of(j * tile, tile), tile)
        product = jnp.dot(panel3[...], across_ref[:, columns], preferred_element_type=jnp.float32)
        out_ref[...] = matrix_ref[...] - product

    @pl.when(first_col)
    def _():
        out_ref[:, :NB] = panel[...]


def update(info, chunks, inv_t, factor, across, matrix, base):
    count = len(chunks)
    width = matrix.shape[1]
    tile = 2 * NB if width % (2 * NB) == 0 else NB
    whole = lambda i, j, info: (0, 0)
    moving = lambda i, j, info: (info[2 + i], j)
    square = pl.BlockSpec((NB, NB), whole)
    in_specs = [square] * (count + 2) + [
        pl.BlockSpec((3 * NB, width), whole),
        pl.BlockSpec((NB, tile), moving),
    ]
    operands = [info, *chunks, inv_t, factor, across, matrix]
    aliases = {}
    if base is not None:
        in_specs.append(ANYWHERE)
        operands.append(base)
        aliases = {len(operands) - 1: 0}
    return pl.pallas_call(
        functools.partial(update_kernel, count, tile),
        grid_spec=pltpu.PrefetchScalarGridSpec(
            num_scalar_prefetch=1,
            grid=(count, width // tile),
            in_specs=in_specs,
            out_specs=pl.BlockSpec((NB, tile), moving),
            scratch_shapes=[
                pltpu.VMEM((NB, NB), jnp.float32),
                pltpu.VMEM((NB, 3 * NB), jnp.bfloat16),
                pltpu.VMEM((NB, 6 * NB), jnp.bfloat16),
                pltpu.VMEM((6 * NB, NB), jnp.bfloat16),
            ],
        ),
        out_shape=jax.ShapeDtypeStruct(matrix.shape, jnp.float32),
        input_output_aliases=aliases,
        compiler_params=PARAMS,
        cost_estimate=pl.CostEstimate(
            flops=6 * count * NB * NB * (width + 2 * NB),
            bytes_accessed=8 * count * NB * width,
            transcendentals=0,
        ),
        name="update_rows",
    )(*operands)


def tree_stages(order):
    reached, done, stages = [0], 0, []
    for bit in order:
        stages.append(([(n, n | bit) for n in reached], bit, done))
        reached = reached + [n | bit for n in reached]
        done |= bit
    return stages


def bits_of(size):
    return [1 << n for n in range(size.bit_length() - 1)]


def corner_orders(rows_axis, cols_axis):
    low = bits_of(cols_axis)
    high = [cols_axis * bit for bit in bits_of(rows_axis)]
    core, across = high[:1], high[:0:-1]
    near, far = low[:1], low[:0:-1]
    return across + near + far + core, far + near + across + core


def spread_apart(held, axis, bit):
    return held + [(n | bit, lax.ppermute(v, axis, [(n, n | bit)])) for n, v in held]


def ring_positions(cols_axis):
    half = cols_axis // 2
    return [2 * n for n in range(half)] + [2 * n + 1 for n in reversed(range(half))]


def scatter_pairs(t, rows_axis, cols_axis):
    pairs = []
    for r in range(cols_axis):
        h, target = divmod(r, rows_axis)
        pairs.append((r, target * cols_axis + h * rows_axis + (target ^ t)))
    return pairs


def ring_shifts(cols_axis):
    shifts = [0]
    last = cols_axis // 2 - 1
    for step in range(1, last):
        shifts += [-step, step]
    return shifts + [cols_axis // 2, -last, last]


def place_table(rows_axis, cols_axis, balanced, row_blocks):
    ring = ring_positions(cols_axis)
    groups = cols_axis // rows_axis
    table = []
    for p in range(rows_axis):
        for q in range(cols_axis):
            if balanced:
                places = []
                for shift in ring_shifts(cols_axis):
                    source = ring[(ring.index(q) + shift) % cols_axis]
                    places.append(groups * ((source % rows_axis) ^ p) + source // rows_axis)
            else:
                places = list(range(row_blocks))
            table.append([p, q] + places)
    return np.array(table, np.int32)


def from_root(value, axis, source):
    kept = jnp.where(lax.axis_index(axis) == source, value, 0).astype(value.dtype)
    return lax.psum(kept, axis)


def tie(*values):
    return lax.optimization_barrier(values)


def on_device(matrix):
    rows_axis = lax.axis_size("row")
    cols_axis = lax.axis_size("col")
    both = ("row", "col")
    index = lax.axis_index("row") * cols_axis + lax.axis_index("col")
    row_blocks = matrix.shape[0] // NB
    col_blocks = matrix.shape[1] // NB
    balanced = row_blocks == cols_axis and col_blocks == rows_axis
    table = jnp.asarray(place_table(rows_axis, cols_axis, balanced, row_blocks))
    places = lax.dynamic_slice_in_dim(table, index, 1, 0)[0]

    parts = list(pack_corner(matrix))
    stages = [tree_stages(order) for order in corner_orders(rows_axis, cols_axis)]
    for step in range(len(stages[0])):
        came = [lax.ppermute(parts[n], both, stages[n][step][0]) for n in range(2)]
        for n in range(2):
            _, bit, done = stages[n][step]
            parts[n] = jnp.where((index & ~done) == bit, came[n], parts[n])
        if step == 0 and balanced:
            parts[0], parts[1], *blocks = tie(*parts, *turn_blocks(matrix, col_blocks))
            pieces = [
                lax.ppermute(blocks[t], both, scatter_pairs(t, rows_axis, cols_axis))
                for t in reversed(range(col_blocks))
            ]
        if step == len(stages[0]) - 2 and balanced:
            parts[0], parts[1], *pieces = tie(*parts, *pieces)
    first_bit, *other_bits = bits_of(rows_axis)[::-1]

    if balanced:
        chunk = functools.reduce(jnp.add, pieces)
        ring = ring_positions(cols_axis)
        up = [(ring[n], ring[(n + 1) % cols_axis]) for n in range(cols_axis)]
        down = [(b, a) for a, b in up]
        over = [(ring[n], ring[(n + cols_axis // 2) % cols_axis]) for n in range(cols_axis)]
        going, coming = [chunk], [chunk]

        def advance():
            going.append(lax.ppermute(going[-1], "col", up))
            coming.append(lax.ppermute(coming[-1], "col", down))

        advance()
        head, chunk = tie(matrix[:NB], chunk)
        held = spread_apart([(0, head)], "row", first_bit)
        parts[0], parts[1], chunk = tie(*parts, chunk)
        work, inv_t = factor_first(*parts)
        work, going[-1], coming[-1], chunk = tie(work, going[-1], coming[-1], chunk)
        advance()
        opposite = lax.ppermute(chunk, "col", over)
        factor, inv, inv_t = factor_last(work, inv_t)
        inv, going[-1], coming[-1], *values = tie(inv, going[-1], coming[-1], *[v for _, v in held])
        held = [(n, v) for (n, _), v in zip(held, values)]
        for _ in range(cols_axis // 2 - 4):
            advance()
        chunks = [chunk]
        for a, b in zip(going[1:], coming[1:]):
            chunks += [a, b]
        advance()
        chunks += [opposite, going[-1], coming[-1]]
        early = len(chunks) - 3
    else:
        column = from_root(matrix[:, :NB], "col", 0)
        chunks = [column[s * NB : (s + 1) * NB] for s in range(row_blocks)]
        factor, inv, inv_t = factor_last(*factor_first(*parts))
        early = len(chunks)
        held = spread_apart([(0, matrix[:NB])], "row", first_bit)

    for bit in other_bits:
        held = spread_apart(held, "row", bit)
    sources = [matrix] + [v for _, v in sorted(held, key=lambda entry: entry[0])][1:]
    across = solve_across(places[:2], inv, sources)
    out = None
    for begin, end in ((0, early), (early, len(chunks))):
        if begin < end:
            info = jnp.concatenate([places[:2], places[2 + begin : 2 + end]])
            out = update(info, chunks[begin:end], inv_t, factor, across, matrix, out)
    return out


def solution(mesh):
    in_specs = (P("row", "col"),)
    out_specs = P("row", "col")
    return jax.shard_map(
        on_device, mesh=mesh, in_specs=in_specs, out_specs=out_specs, check_vma=False
    )
```

```python
import functools

import jax
import jax.numpy as jnp
import numpy as np
from jax import lax
from jax.experimental import pallas as pl
from jax.experimental.pallas import tpu as pltpu
from jax.sharding import PartitionSpec as P

NB = 512
SUB = 128
LANES = 8
COUNT = NB // SUB
VMEM_BYTES = 60 * 1024 * 1024
LOWER = [(i, j) for i in range(COUNT) for j in range(i + 1)]
HALF = len(LOWER) // 2
EXACT = lax.Precision.HIGHEST
PARAMS = pltpu.CompilerParams(vmem_limit_bytes=VMEM_BYTES)
SQUARE = jax.ShapeDtypeStruct((NB, NB), jnp.float32)
IN_VMEM = pl.BlockSpec(memory_space=pltpu.VMEM)
ANYWHERE = pl.BlockSpec(memory_space=pl.ANY)


def dot_nt(a, b):
    return lax.dot_general(
        a, b, (((1,), (1,)), ((), ())), precision=EXACT, preferred_element_type=jnp.float32
    )


def dot_nn(a, b):
    return lax.dot_general(
        a, b, (((1,), (0,)), ((), ())), precision=EXACT, preferred_element_type=jnp.float32
    )


def split2(value):
    high = value.astype(jnp.bfloat16)
    low = (value - high.astype(jnp.float32)).astype(jnp.bfloat16)
    return high, low


def split3(value):
    high = value.astype(jnp.bfloat16)
    rest = value - high.astype(jnp.float32)
    middle, low = split2(rest)
    return high, middle, low


def store_parts(ref, value, axis, pattern):
    parts = split3(value)
    half = NB // 2
    for h in range(2):
        for n, k in enumerate(pattern):
            begin = (h * len(pattern) + n) * half
            if axis:
                ref[:, begin : begin + half] = parts[k][:, h * half : (h + 1) * half]
            else:
                ref[begin : begin + half] = parts[k][h * half : (h + 1) * half]


LEFT_PARTS = (0, 1, 2, 0, 1, 0)
RIGHT_PARTS = (0, 0, 0, 1, 1, 2)
DEPTH = len(LEFT_PARTS) * NB


def pack_kernel(matrix_ref, first_ref, second_ref):
    for n, (i, j) in enumerate(LOWER):
        target, place = (first_ref, n) if n < HALF else (second_ref, n - HALF)
        target[place] = matrix_ref[i * SUB : (i + 1) * SUB, j * SUB : (j + 1) * SUB]


def pack_corner(matrix):
    part = jax.ShapeDtypeStruct((HALF, SUB, SUB), jnp.float32)
    whole = pl.BlockSpec((HALF, SUB, SUB), lambda i: (0, 0, 0))
    return pl.pallas_call(
        pack_kernel,
        grid=(1,),
        out_shape=(part, part),
        in_specs=[pl.BlockSpec((NB, NB), lambda i: (0, 0))],
        out_specs=(whole, whole),
        compiler_params=PARAMS,
        name="pack_corner",
    )(matrix)


def turn_kernel(count, matrix_ref, *refs):
    for t in range(count):
        refs[t][...] = matrix_ref[:, t * NB : (t + 1) * NB].T
    refs[count][...] = matrix_ref[...]


def turn_blocks(matrix, count):
    square = pl.BlockSpec((NB, NB), lambda i: (0, 0))
    return pl.pallas_call(
        functools.partial(turn_kernel, count),
        grid=(1,),
        out_shape=(SQUARE,) * count + (jax.ShapeDtypeStruct((NB, count * NB), jnp.float32),),
        in_specs=[pl.BlockSpec((NB, count * NB), lambda i: (0, 0))],
        out_specs=(square,) * count + (pl.BlockSpec((NB, count * NB), lambda i: (0, 0)),),
        compiler_params=PARAMS,
        name="turn_blocks",
    )(matrix)


def reciprocal(value):
    guess = pl.reciprocal(value, approx=True)
    guess = guess * (2.0 - value * guess)
    return guess * (2.0 - value * guess)


def small_cholesky(block):
    groups = SUB // LANES
    shape = (LANES, SUB)
    lane = lax.broadcasted_iota(jnp.int32, shape, 1)
    sub = lax.broadcasted_iota(jnp.int32, shape, 0)
    left = [block[g * LANES : (g + 1) * LANES] for g in range(groups)]
    right = [jnp.where(lane == sub + g * LANES, 1.0, 0.0) for g in range(groups)]
    for g0 in range(groups):
        i = g0 * LANES
        head, side = left[g0], right[g0]
        columns = [jnp.broadcast_to(head[:, i + j : i + j + 1], shape) for j in range(LANES)]
        ratios, heads, sides = [], [], []
        for k in range(LANES):
            inverse = reciprocal(columns[k][k : k + 1])
            ratio = {j: columns[j][k : k + 1] * inverse for j in range(k + 1, LANES)}
            scaled_head = head[k : k + 1] * inverse
            scaled_side = side[k : k + 1] * inverse
            ratios.append(ratio)
            heads.append(scaled_head)
            sides.append(scaled_side)
            if k + 1 < LANES:
                below = jnp.where(sub > k, columns[k], 0.0)
                for j in range(k + 1, LANES):
                    columns[j] = columns[j] - below * ratio[j]
                head = head - below * scaled_head
                side = side - below * scaled_side
        left[g0], right[g0] = head, side
        for g in range(g0 + 1, groups):
            own = [jnp.broadcast_to(left[g][:, i + j : i + j + 1], shape) for j in range(LANES)]
            body, tail = left[g], right[g]
            for k in range(LANES):
                for j in range(k + 1, LANES):
                    own[j] = own[j] - own[k] * ratios[k][j]
                body = body - own[k] * heads[k]
                tail = tail - own[k] * sides[k]
            left[g], right[g] = body, tail
    upper, inverse = [], []
    for g in range(groups):
        row = sub + g * LANES
        pivot = jnp.sum(jnp.where(lane == row, left[g], 0.0), axis=1, keepdims=True)
        scale = lax.rsqrt(pivot)
        upper.append(jnp.where(lane >= row, left[g] * scale, 0.0))
        inverse.append(jnp.where(lane <= row, right[g] * scale, 0.0))
    return jnp.concatenate(upper, 0), jnp.concatenate(inverse, 0)


def factor_block(k, work, inv_t):
    start = pl.multiple_of(k * SUB, SUB)
    here = pl.ds(start, SUB)
    upper, inverse = small_cholesky(work[here, here])
    inverse_t = inverse.T
    row = lax.broadcasted_iota(jnp.int32, (NB, SUB), 0)
    panel = jnp.where(row >= start + SUB, dot_nn(work[:, here], inverse_t), 0.0)
    work[...] -= dot_nt(panel, panel)
    work[:, here] = panel
    work[here, here] = upper.T
    column = lax.broadcasted_iota(jnp.int32, (SUB, NB), 1)
    before = jnp.where(column < start, work[here, :], 0.0)
    inv_t[:, here] = -dot_nn(dot_nt(inv_t[...], before), inverse_t)
    inv_t[here, here] = inverse_t


def factor_first_kernel(last, first_ref, second_ref, work, inv_t):
    inv_t[...] = jnp.zeros_like(inv_t)
    work[...] = jnp.zeros_like(work)
    for n, (i, j) in enumerate(LOWER):
        value = first_ref[n] if n < HALF else second_ref[n - HALF]
        work[i * SUB : (i + 1) * SUB, j * SUB : (j + 1) * SUB] = value

    @pl.loop(0, last)
    def _(k):
        factor_block(k, work, inv_t)


def factor_last_kernel(begin, work_in, inv_t_in, factor_ref, inv_ref, inv_t_ref):
    factor_ref[...] = work_in[...]
    inv_t_ref[...] = inv_t_in[...]

    @pl.loop(begin, COUNT)
    def _(k):
        factor_block(k, factor_ref, inv_t_ref)

    inv_ref[...] = inv_t_ref[...].T


FACTOR_COST = pl.CostEstimate(flops=2 * NB**3, bytes_accessed=4 * NB * NB * 4, transcendentals=0)


def factor_first(first, second):
    return pl.pallas_call(
        functools.partial(factor_first_kernel, COUNT // 2),
        out_shape=(SQUARE, SQUARE),
        in_specs=[IN_VMEM] * 2,
        out_specs=(IN_VMEM,) * 2,
        compiler_params=PARAMS,
        cost_estimate=FACTOR_COST,
        name="factor_first",
    )(first, second)


def factor_last(work, inv_t):
    return pl.pallas_call(
        functools.partial(factor_last_kernel, COUNT // 2),
        out_shape=(SQUARE, SQUARE, SQUARE),
        in_specs=[IN_VMEM] * 2,
        out_specs=(IN_VMEM,) * 3,
        compiler_params=PARAMS,
        cost_estimate=FACTOR_COST,
        name="factor_last",
    )(work, inv_t)


def update_kernel(count, ahead, offset, tile, source_count, info, *refs):
    factor_ref, inv_ref, inv_t_ref, matrix_ref = refs[:4]
    chunks = refs[4 : 4 + count]
    sources = refs[4 + count : 4 + count + source_count]
    out_ref = refs[-12 - ahead]
    across, rows, arrived, panel, panel3, left, right = refs[-11:-4]
    chunk_sems, row_sems, across_sem, out_sem = refs[-4:]
    i, j = pl.program_id(0), pl.program_id(1)
    tiles = across.shape[1] // tile
    half, deep = NB // 2, DEPTH // 2
    first_row = jnp.logical_and(info[0] == 0, info[2 + offset + jnp.maximum(i - ahead, 0)] == 0)
    first_col = jnp.logical_and(info[1] == 0, j == 0)

    def chunk_copy(n):
        return pltpu.make_async_copy(chunks[n], arrived.at[n], chunk_sems.at[n])

    def row_copy(n, t):
        place = pl.ds(t * tile, tile)
        return pltpu.make_async_copy(
            sources[n].at[pl.ds(0, NB), place], rows.at[:, place], row_sems.at[t]
        )

    @pl.when(jnp.logical_and(i == 0, j == 0))
    def _():
        if ahead:
            for n in range(source_count):

                @pl.when(info[0] == n)
                def _():
                    for t in range(tiles):
                        row_copy(n, t).start()

        for n in range(count):
            chunk_copy(n).start()
        if ahead:
            store_parts(left, inv_ref[...], 1, LEFT_PARTS)
        else:
            pltpu.make_async_copy(sources[0], across, across_sem).start()

    if ahead:

        @pl.when(i == 0)
        def _():
            for t in range(tiles):

                @pl.when(j == t)
                def _():
                    row_copy(0, t).wait()
                    for c in range(t * tile, (t + 1) * tile, NB):
                        store_parts(right, rows[:, c : c + NB], 0, RIGHT_PARTS)
                        for h in range(2):
                            part = slice(h * half, (h + 1) * half)
                            value = jnp.dot(
                                left[part, : (h + 1) * deep],
                                right[: (h + 1) * deep],
                                preferred_element_type=jnp.float32,
                            )
                            high, low = split2(value)
                            across[h * half : (h + 1) * half, c : c + NB] = high
                            across[NB + h * half : NB + (h + 1) * half, c : c + NB] = high
                            across[2 * NB + h * half : 2 * NB + (h + 1) * half, c : c + NB] = low

        handed = pltpu.make_async_copy(across, refs[-12], out_sem)

        @pl.when(jnp.logical_and(i == 1, j == 0))
        def _():
            handed.start()

        @pl.when(jnp.logical_and(i == count, j == tiles - 1))
        def _():
            handed.wait()

    @pl.when(jnp.logical_and(i == ahead, j == 0))
    def _():
        store_parts(right, inv_t_ref[...], 0, RIGHT_PARTS)

    @pl.when(jnp.logical_and(i >= ahead, j == 0))
    def _():
        for n in range(count):

            @pl.when(i == n + ahead)
            def _():
                chunk_copy(n).wait()
                store_parts(left, arrived[n], 1, LEFT_PARTS)

        for h in range(2):
            part = slice(h * half, (h + 1) * half)
            value = jnp.dot(
                left[:, : (h + 1) * deep],
                right[: (h + 1) * deep, part],
                preferred_element_type=jnp.float32,
            )
            panel[:, part] = value
            high, low = split2(value)
            panel3[:, h * half : (h + 1) * half] = high
            panel3[:, NB + h * half : NB + (h + 1) * half] = low
            panel3[:, 2 * NB + h * half : 2 * NB + (h + 1) * half] = high

        @pl.when(first_row)
        def _():
            panel[...] = factor_ref[...]

    if not ahead:

        @pl.when(jnp.logical_and(i == 0, j == 0))
        def _():
            pltpu.make_async_copy(sources[0], across, across_sem).wait()

    @pl.when(jnp.logical_and(i >= ahead, first_row))
    def _():
        out_ref[...] = jnp.zeros_like(out_ref)

    @pl.when(jnp.logical_and(i >= ahead, jnp.logical_not(first_row)))
    def _():
        columns = pl.ds(pl.multiple_of(j * tile, tile), tile)
        product = jnp.dot(panel3[...], across[:, columns], preferred_element_type=jnp.float32)
        out_ref[...] = matrix_ref[...] - product

    @pl.when(jnp.logical_and(i >= ahead, first_col))
    def _():
        out_ref[:, :NB] = panel[...]


def update(info, offset, chunks, factor, inv, inv_t, matrix, sources, base):
    count = len(chunks)
    ahead = 1 if base is None else 0
    width = matrix.shape[1]
    tile = 2 * NB if width % (2 * NB) == 0 else NB
    whole = lambda i, j, info: (0, 0)

    def moving(i, j, info):
        n = i - ahead
        return info[2 + offset + jnp.maximum(n, 0)], jnp.where(n < 0, 0, j)

    square = pl.BlockSpec((NB, NB), whole)
    block = pl.BlockSpec((NB, tile), moving)
    across = jax.ShapeDtypeStruct((3 * NB, width), jnp.bfloat16)
    in_specs = [square] * 3 + [block] + [ANYWHERE] * (count + len(sources))
    operands = [info, factor, inv, inv_t, matrix, *chunks, *sources]
    out_shape, out_specs, aliases = [jax.ShapeDtypeStruct(matrix.shape, jnp.float32)], [block], {}
    if ahead:
        out_shape.append(across)
        out_specs.append(ANYWHERE)
    else:
        in_specs.append(ANYWHERE)
        operands.append(base)
        aliases = {len(operands) - 1: 0}
    return pl.pallas_call(
        functools.partial(update_kernel, count, ahead, offset, tile, len(sources)),
        grid_spec=pltpu.PrefetchScalarGridSpec(
            num_scalar_prefetch=1,
            grid=(count + ahead, width // tile),
            in_specs=in_specs,
            out_specs=out_specs,
            scratch_shapes=[
                pltpu.VMEM(across.shape, jnp.bfloat16),
                pltpu.VMEM((NB, width) if ahead else (8, 128), jnp.float32),
                pltpu.VMEM((count, NB, NB), jnp.float32),
                pltpu.VMEM((NB, NB), jnp.float32),
                pltpu.VMEM((NB, 3 * NB), jnp.bfloat16),
                pltpu.VMEM((NB, DEPTH), jnp.bfloat16),
                pltpu.VMEM((DEPTH, NB), jnp.bfloat16),
                pltpu.SemaphoreType.DMA((count,)),
                pltpu.SemaphoreType.DMA((width // tile,)),
                pltpu.SemaphoreType.DMA,
                pltpu.SemaphoreType.DMA,
            ],
        ),
        out_shape=out_shape,
        input_output_aliases=aliases,
        compiler_params=PARAMS,
        cost_estimate=pl.CostEstimate(
            flops=6 * (count + ahead) * NB * NB * (width + 2 * NB),
            bytes_accessed=8 * count * NB * width,
            transcendentals=0,
        ),
        name="update_rows",
    )(*operands)


def tree_stages(order):
    reached, done, stages = [0], 0, []
    for bit in order:
        stages.append(([(n, n | bit) for n in reached], bit, done))
        reached = reached + [n | bit for n in reached]
        done |= bit
    return stages


def bits_of(size):
    return [1 << n for n in range(size.bit_length() - 1)]


def corner_orders(rows_axis, cols_axis):
    low = bits_of(cols_axis)
    high = [cols_axis * bit for bit in bits_of(rows_axis)]
    core, across = high[:1], high[:0:-1]
    near, far = low[:1], low[:0:-1]
    return across + near + far + core, far + near + across + core


def spread_apart(held, axis, bit):
    return held + [(n | bit, lax.ppermute(v, axis, [(n, n | bit)])) for n, v in held]


def ring_positions(cols_axis):
    half = cols_axis // 2
    return [2 * n for n in range(half)] + [2 * n + 1 for n in reversed(range(half))]


def scatter_pairs(t, rows_axis, cols_axis):
    pairs = []
    for r in range(cols_axis):
        h, target = divmod(r, rows_axis)
        pairs.append((r, target * cols_axis + h * rows_axis + (target ^ t)))
    return pairs


def ring_shifts(cols_axis):
    shifts = [0]
    last = cols_axis // 2 - 1
    for step in range(1, last):
        shifts += [-step, step]
    return shifts + [cols_axis // 2, -last, last]


def place_table(rows_axis, cols_axis, balanced, row_blocks):
    ring = ring_positions(cols_axis)
    groups = cols_axis // rows_axis
    table = []
    for p in range(rows_axis):
        for q in range(cols_axis):
            if balanced:
                places = []
                for shift in ring_shifts(cols_axis):
                    source = ring[(ring.index(q) + shift) % cols_axis]
                    places.append(groups * ((source % rows_axis) ^ p) + source // rows_axis)
            else:
                places = list(range(row_blocks))
            table.append([p, q] + places)
    return np.array(table, np.int32)


def from_root(value, axis, source):
    kept = jnp.where(lax.axis_index(axis) == source, value, 0).astype(value.dtype)
    return lax.psum(kept, axis)


def tie(*values):
    return lax.optimization_barrier(values)


def on_device(matrix):
    rows_axis = lax.axis_size("row")
    cols_axis = lax.axis_size("col")
    both = ("row", "col")
    index = lax.axis_index("row") * cols_axis + lax.axis_index("col")
    row_blocks = matrix.shape[0] // NB
    col_blocks = matrix.shape[1] // NB
    balanced = row_blocks == cols_axis and col_blocks == rows_axis
    table = jnp.asarray(place_table(rows_axis, cols_axis, balanced, row_blocks))
    places = lax.dynamic_slice_in_dim(table, index, 1, 0)[0]

    parts = list(pack_corner(matrix))
    stages = [tree_stages(order) for order in corner_orders(rows_axis, cols_axis)]
    *blocks, head = turn_blocks(matrix, col_blocks)
    pieces = []
    if balanced:
        pieces = [
            lax.ppermute(blocks[t], both, scatter_pairs(t, rows_axis, cols_axis))
            for t in reversed(range(col_blocks))
        ]
    for step in range(len(stages[0])):
        if step == len(stages[0]) - 1:
            parts[0], parts[1], *pieces = tie(*parts, *pieces)
        came = [lax.ppermute(parts[n], both, stages[n][step][0]) for n in range(2)]
        for n in range(2):
            _, bit, done = stages[n][step]
            parts[n] = jnp.where((index & ~done) == bit, came[n], parts[n])
    first_bit, *other_bits = bits_of(rows_axis)[::-1]

    if balanced:
        chunk = functools.reduce(jnp.add, pieces)
        ring = ring_positions(cols_axis)
        up = [(ring[n], ring[(n + 1) % cols_axis]) for n in range(cols_axis)]
        down = [(b, a) for a, b in up]
        over = [(ring[n], ring[(n + cols_axis // 2) % cols_axis]) for n in range(cols_axis)]
        going, coming = [chunk], [chunk]

        def advance():
            going.append(lax.ppermute(going[-1], "col", up))
            coming.append(lax.ppermute(coming[-1], "col", down))

        advance()
        head, chunk = tie(head, chunk)
        held = spread_apart([(0, head)], "row", first_bit)
        own = [(n, head) for n in (0,)]
        for bit in other_bits:
            own = spread_apart(own, "row", bit)
        parts[0], parts[1], chunk = tie(*parts, chunk)
        work, inv_t = factor_first(*parts)
        work, going[-1], coming[-1], chunk = tie(work, going[-1], coming[-1], chunk)
        advance()
        opposite = lax.ppermute(chunk, "col", over)
        factor, inv, inv_t = factor_last(work, inv_t)
        far, value = held[1]
        inv, going[-1], coming[-1], value, opposite = tie(inv, going[-1], coming[-1], value, opposite)
        far = [(far, value)]
        for bit in other_bits:
            far = spread_apart(far, "row", bit)
        held = own + far
        for _ in range(cols_axis // 2 - 4):
            advance()
        chunks = [chunk]
        for a, b in zip(going[1:], coming[1:]):
            chunks += [a, b]
        advance()
        chunks += [opposite, going[-1], coming[-1]]
        early = len(chunks) - 3
    else:
        column = from_root(matrix[:, :NB], "col", 0)
        chunks = [column[s * NB : (s + 1) * NB] for s in range(row_blocks)]
        factor, inv, inv_t = factor_last(*factor_first(*parts))
        early = len(chunks)
        held = [(0, head)]
        for bit in [first_bit, *other_bits]:
            held = spread_apart(held, "row", bit)

    sources = [matrix] + [v for _, v in sorted(held, key=lambda entry: entry[0])][1:]
    out, across = update(places, 0, chunks[:early], factor, inv, inv_t, matrix, sources, None)
    if early < len(chunks):
        (out,) = update(places, early, chunks[early:], factor, inv, inv_t, matrix, [across], out)
    return out


def solution(mesh):
    in_specs = (P("row", "col"),)
    out_specs = P("row", "col")
    return jax.shard_map(
        on_device, mesh=mesh, in_specs=in_specs, out_specs=out_specs, check_vma=False
    )
```

```python
import functools

import jax
import jax.numpy as jnp
import numpy as np
from jax import lax
from jax.experimental import pallas as pl
from jax.experimental.pallas import tpu as pltpu
from jax.sharding import PartitionSpec as P

NB = 512
SUB = 128
LANES = 8
COUNT = NB // SUB
VMEM_BYTES = 60 * 1024 * 1024
LOWER = [(i, j) for i in range(COUNT) for j in range(i + 1)]
HALF = len(LOWER) // 2
EXACT = lax.Precision.HIGHEST
PARAMS = pltpu.CompilerParams(vmem_limit_bytes=VMEM_BYTES)
SQUARE = jax.ShapeDtypeStruct((NB, NB), jnp.float32)
IN_VMEM = pl.BlockSpec(memory_space=pltpu.VMEM)
ANYWHERE = pl.BlockSpec(memory_space=pl.ANY)


def dot_nt(a, b):
    return lax.dot_general(
        a, b, (((1,), (1,)), ((), ())), precision=EXACT, preferred_element_type=jnp.float32
    )


def dot_nn(a, b):
    return lax.dot_general(
        a, b, (((1,), (0,)), ((), ())), precision=EXACT, preferred_element_type=jnp.float32
    )


def split2(value):
    high = value.astype(jnp.bfloat16)
    low = (value - high.astype(jnp.float32)).astype(jnp.bfloat16)
    return high, low


def split3(value):
    high = value.astype(jnp.bfloat16)
    rest = value - high.astype(jnp.float32)
    middle, low = split2(rest)
    return high, middle, low


def store_parts(ref, value, axis, pattern):
    parts = split3(value)
    half = NB // 2
    for h in range(2):
        for n, k in enumerate(pattern):
            begin = (h * len(pattern) + n) * half
            if axis:
                ref[:, begin : begin + half] = parts[k][:, h * half : (h + 1) * half]
            else:
                ref[begin : begin + half] = parts[k][h * half : (h + 1) * half]


LEFT_PARTS = (0, 1, 2, 0, 1, 0)
RIGHT_PARTS = (0, 0, 0, 1, 1, 2)
DEPTH = len(LEFT_PARTS) * NB


def pack_kernel(matrix_ref, first_ref, second_ref):
    for n, (i, j) in enumerate(LOWER):
        target, place = (first_ref, n) if n < HALF else (second_ref, n - HALF)
        target[place] = matrix_ref[i * SUB : (i + 1) * SUB, j * SUB : (j + 1) * SUB]


def pack_corner(matrix):
    part = jax.ShapeDtypeStruct((HALF, SUB, SUB), jnp.float32)
    whole = pl.BlockSpec((HALF, SUB, SUB), lambda i: (0, 0, 0))
    return pl.pallas_call(
        pack_kernel,
        grid=(1,),
        out_shape=(part, part),
        in_specs=[pl.BlockSpec((NB, NB), lambda i: (0, 0))],
        out_specs=(whole, whole),
        compiler_params=PARAMS,
        name="pack_corner",
    )(matrix)


def turn_kernel(count, matrix_ref, *refs):
    for t in range(count):
        refs[t][...] = matrix_ref[:, t * NB : (t + 1) * NB].T
    refs[count][...] = matrix_ref[...]


def turn_blocks(matrix, count):
    square = pl.BlockSpec((NB, NB), lambda i: (0, 0))
    return pl.pallas_call(
        functools.partial(turn_kernel, count),
        grid=(1,),
        out_shape=(SQUARE,) * count + (jax.ShapeDtypeStruct((NB, count * NB), jnp.float32),),
        in_specs=[pl.BlockSpec((NB, count * NB), lambda i: (0, 0))],
        out_specs=(square,) * count + (pl.BlockSpec((NB, count * NB), lambda i: (0, 0)),),
        compiler_params=PARAMS,
        name="turn_blocks",
    )(matrix)


def reciprocal(value):
    guess = pl.reciprocal(value, approx=True)
    return guess * (2.0 - value * guess)


def small_cholesky(block):
    groups = SUB // LANES
    shape = (LANES, SUB)
    lane = lax.broadcasted_iota(jnp.int32, shape, 1)
    sub = lax.broadcasted_iota(jnp.int32, shape, 0)
    left = [block[g * LANES : (g + 1) * LANES] for g in range(groups)]
    right = [jnp.where(lane == sub + g * LANES, 1.0, 0.0) for g in range(groups)]
    for g0 in range(groups):
        i = g0 * LANES
        head, side = left[g0], right[g0]
        columns = [jnp.broadcast_to(head[:, i + j : i + j + 1], shape) for j in range(LANES)]
        ratios, heads, sides = [], [], []
        for k in range(LANES):
            inverse = reciprocal(columns[k][k : k + 1])
            ratio = {j: columns[j][k : k + 1] * inverse for j in range(k + 1, LANES)}
            scaled_head = head[k : k + 1] * inverse
            scaled_side = side[k : k + 1] * inverse
            ratios.append(ratio)
            heads.append(scaled_head)
            sides.append(scaled_side)
            if k + 1 < LANES:
                below = jnp.where(sub > k, columns[k], 0.0)
                for j in range(k + 1, LANES):
                    columns[j] = columns[j] - below * ratio[j]
                head = head - below * scaled_head
                side = side - below * scaled_side
        left[g0], right[g0] = head, side
        for g in range(g0 + 1, groups):
            own = [jnp.broadcast_to(left[g][:, i + j : i + j + 1], shape) for j in range(LANES)]
            body, tail = left[g], right[g]
            for k in range(LANES):
                for j in range(k + 1, LANES):
                    own[j] = own[j] - own[k] * ratios[k][j]
                body = body - own[k] * heads[k]
                tail = tail - own[k] * sides[k]
            left[g], right[g] = body, tail
    upper, inverse = [], []
    for g in range(groups):
        row = sub + g * LANES
        pivot = jnp.sum(jnp.where(lane == row, left[g], 0.0), axis=1, keepdims=True)
        scale = lax.rsqrt(pivot)
        upper.append(jnp.where(lane >= row, left[g] * scale, 0.0))
        inverse.append(jnp.where(lane <= row, right[g] * scale, 0.0))
    return jnp.concatenate(upper, 0), jnp.concatenate(inverse, 0)


def factor_block(k, work, inv_t):
    start = pl.multiple_of(k * SUB, SUB)
    here = pl.ds(start, SUB)
    upper, inverse = small_cholesky(work[here, here])
    inverse_t = inverse.T
    row = lax.broadcasted_iota(jnp.int32, (NB, SUB), 0)
    panel = jnp.where(row >= start + SUB, dot_nn(work[:, here], inverse_t), 0.0)
    work[...] -= dot_nt(panel, panel)
    work[:, here] = panel
    work[here, here] = upper.T
    column = lax.broadcasted_iota(jnp.int32, (SUB, NB), 1)
    before = jnp.where(column < start, work[here, :], 0.0)
    inv_t[:, here] = -dot_nn(dot_nt(inv_t[...], before), inverse_t)
    inv_t[here, here] = inverse_t


def factor_first_kernel(last, first_ref, second_ref, work, inv_t):
    inv_t[...] = jnp.zeros_like(inv_t)
    work[...] = jnp.zeros_like(work)
    for n, (i, j) in enumerate(LOWER):
        value = first_ref[n] if n < HALF else second_ref[n - HALF]
        work[i * SUB : (i + 1) * SUB, j * SUB : (j + 1) * SUB] = value

    @pl.loop(0, last)
    def _(k):
        factor_block(k, work, inv_t)


def factor_last_kernel(begin, work_in, inv_t_in, factor_ref, inv_ref, inv_t_ref):
    factor_ref[...] = work_in[...]
    inv_t_ref[...] = inv_t_in[...]

    @pl.loop(begin, COUNT)
    def _(k):
        factor_block(k, factor_ref, inv_t_ref)

    inv_ref[...] = inv_t_ref[...].T


FACTOR_COST = pl.CostEstimate(flops=2 * NB**3, bytes_accessed=4 * NB * NB * 4, transcendentals=0)


def factor_first(first, second):
    return pl.pallas_call(
        functools.partial(factor_first_kernel, COUNT // 2),
        out_shape=(SQUARE, SQUARE),
        in_specs=[IN_VMEM] * 2,
        out_specs=(IN_VMEM,) * 2,
        compiler_params=PARAMS,
        cost_estimate=FACTOR_COST,
        name="factor_first",
    )(first, second)


def factor_last(work, inv_t):
    return pl.pallas_call(
        functools.partial(factor_last_kernel, COUNT // 2),
        out_shape=(SQUARE, SQUARE, SQUARE),
        in_specs=[IN_VMEM] * 2,
        out_specs=(IN_VMEM,) * 3,
        compiler_params=PARAMS,
        cost_estimate=FACTOR_COST,
        name="factor_last",
    )(work, inv_t)


def update_kernel(count, ahead, offset, tile, source_count, info, *refs):
    factor_ref, inv_ref, inv_t_ref, matrix_ref = refs[:4]
    chunks = refs[4 : 4 + count]
    sources = refs[4 + count : 4 + count + source_count]
    out_ref = refs[-12 - ahead]
    across, rows, arrived, panel, panel3, left, right = refs[-11:-4]
    chunk_sems, row_sems, across_sem, out_sem = refs[-4:]
    i, j = pl.program_id(0), pl.program_id(1)
    tiles = across.shape[1] // tile
    half, deep = NB // 2, DEPTH // 2
    first_row = jnp.logical_and(info[0] == 0, info[2 + offset + jnp.maximum(i - ahead, 0)] == 0)
    first_col = jnp.logical_and(info[1] == 0, j == 0)

    def chunk_copy(n):
        return pltpu.make_async_copy(chunks[n], arrived.at[n], chunk_sems.at[n])

    def row_copy(n, t):
        place = pl.ds(t * tile, tile)
        return pltpu.make_async_copy(
            sources[n].at[pl.ds(0, NB), place], rows.at[:, place], row_sems.at[t]
        )

    @pl.when(jnp.logical_and(i == 0, j == 0))
    def _():
        if ahead:
            for n in range(source_count):

                @pl.when(info[0] == n)
                def _():
                    for t in range(tiles):
                        row_copy(n, t).start()

        for n in range(count):
            chunk_copy(n).start()
        if ahead:
            store_parts(left, inv_ref[...], 1, LEFT_PARTS)
        else:
            pltpu.make_async_copy(sources[0], across, across_sem).start()

    if ahead:

        @pl.when(i == 0)
        def _():
            for t in range(tiles):

                @pl.when(j == t)
                def _():
                    row_copy(0, t).wait()
                    for c in range(t * tile, (t + 1) * tile, NB):
                        store_parts(right, rows[:, c : c + NB], 0, RIGHT_PARTS)
                        for h in range(2):
                            part = slice(h * half, (h + 1) * half)
                            value = jnp.dot(
                                left[part, : (h + 1) * deep],
                                right[: (h + 1) * deep],
                                preferred_element_type=jnp.float32,
                            )
                            high, low = split2(value)
                            across[h * half : (h + 1) * half, c : c + NB] = high
                            across[NB + h * half : NB + (h + 1) * half, c : c + NB] = high
                            across[2 * NB + h * half : 2 * NB + (h + 1) * half, c : c + NB] = low

        handed = pltpu.make_async_copy(across, refs[-12], out_sem)

        @pl.when(jnp.logical_and(i == 1, j == 0))
        def _():
            handed.start()

        @pl.when(jnp.logical_and(i == count, j == tiles - 1))
        def _():
            handed.wait()

    @pl.when(jnp.logical_and(i == ahead, j == 0))
    def _():
        store_parts(right, inv_t_ref[...], 0, RIGHT_PARTS)

    @pl.when(jnp.logical_and(i >= ahead, j == 0))
    def _():
        for n in range(count):

            @pl.when(i == n + ahead)
            def _():
                chunk_copy(n).wait()
                store_parts(left, arrived[n], 1, LEFT_PARTS)

        for h in range(2):
            part = slice(h * half, (h + 1) * half)
            value = jnp.dot(
                left[:, : (h + 1) * deep],
                right[: (h + 1) * deep, part],
                preferred_element_type=jnp.float32,
            )
            panel[:, part] = value
            high, low = split2(value)
            panel3[:, h * half : (h + 1) * half] = high
            panel3[:, NB + h * half : NB + (h + 1) * half] = low
            panel3[:, 2 * NB + h * half : 2 * NB + (h + 1) * half] = high

        @pl.when(first_row)
        def _():
            panel[...] = factor_ref[...]

    if not ahead:

        @pl.when(jnp.logical_and(i == 0, j == 0))
        def _():
            pltpu.make_async_copy(sources[0], across, across_sem).wait()

    @pl.when(jnp.logical_and(i >= ahead, first_row))
    def _():
        out_ref[...] = jnp.zeros_like(out_ref)

    @pl.when(jnp.logical_and(i >= ahead, jnp.logical_not(first_row)))
    def _():
        columns = pl.ds(pl.multiple_of(j * tile, tile), tile)
        product = jnp.dot(panel3[...], across[:, columns], preferred_element_type=jnp.float32)
        out_ref[...] = matrix_ref[...] - product

    @pl.when(jnp.logical_and(i >= ahead, first_col))
    def _():
        out_ref[:, :NB] = panel[...]


def update(info, offset, chunks, factor, inv, inv_t, matrix, sources, base):
    count = len(chunks)
    ahead = 1 if base is None else 0
    width = matrix.shape[1]
    tile = 2 * NB if width % (2 * NB) == 0 else NB
    whole = lambda i, j, info: (0, 0)

    def moving(i, j, info):
        n = i - ahead
        return info[2 + offset + jnp.maximum(n, 0)], jnp.where(n < 0, 0, j)

    square = pl.BlockSpec((NB, NB), whole)
    block = pl.BlockSpec((NB, tile), moving)
    across = jax.ShapeDtypeStruct((3 * NB, width), jnp.bfloat16)
    in_specs = [square] * 3 + [block] + [ANYWHERE] * (count + len(sources))
    operands = [info, factor, inv, inv_t, matrix, *chunks, *sources]
    out_shape, out_specs, aliases = [jax.ShapeDtypeStruct(matrix.shape, jnp.float32)], [block], {}
    if ahead:
        out_shape.append(across)
        out_specs.append(ANYWHERE)
    else:
        in_specs.append(ANYWHERE)
        operands.append(base)
        aliases = {len(operands) - 1: 0}
    return pl.pallas_call(
        functools.partial(update_kernel, count, ahead, offset, tile, len(sources)),
        grid_spec=pltpu.PrefetchScalarGridSpec(
            num_scalar_prefetch=1,
            grid=(count + ahead, width // tile),
            in_specs=in_specs,
            out_specs=out_specs,
            scratch_shapes=[
                pltpu.VMEM(across.shape, jnp.bfloat16),
                pltpu.VMEM((NB, width) if ahead else (8, 128), jnp.float32),
                pltpu.VMEM((count, NB, NB), jnp.float32),
                pltpu.VMEM((NB, NB), jnp.float32),
                pltpu.VMEM((NB, 3 * NB), jnp.bfloat16),
                pltpu.VMEM((NB, DEPTH), jnp.bfloat16),
                pltpu.VMEM((DEPTH, NB), jnp.bfloat16),
                pltpu.SemaphoreType.DMA((count,)),
                pltpu.SemaphoreType.DMA((width // tile,)),
                pltpu.SemaphoreType.DMA,
                pltpu.SemaphoreType.DMA,
            ],
        ),
        out_shape=out_shape,
        input_output_aliases=aliases,
        compiler_params=PARAMS,
        cost_estimate=pl.CostEstimate(
            flops=6 * (count + ahead) * NB * NB * (width + 2 * NB),
            bytes_accessed=8 * count * NB * width,
            transcendentals=0,
        ),
        name="update_rows",
    )(*operands)


def tree_stages(order):
    reached, done, stages = [0], 0, []
    for bit in order:
        stages.append(([(n, n | bit) for n in reached], bit, done))
        reached = reached + [n | bit for n in reached]
        done |= bit
    return stages


def bits_of(size):
    return [1 << n for n in range(size.bit_length() - 1)]


def corner_orders(rows_axis, cols_axis):
    low = bits_of(cols_axis)
    high = [cols_axis * bit for bit in bits_of(rows_axis)]
    core, across = high[:1], high[:0:-1]
    near, far = low[:1], low[:0:-1]
    return across + near + far + core, far + near + across + core


def spread_apart(held, axis, bit):
    return held + [(n | bit, lax.ppermute(v, axis, [(n, n | bit)])) for n, v in held]


def ring_positions(cols_axis):
    half = cols_axis // 2
    return [2 * n for n in range(half)] + [2 * n + 1 for n in reversed(range(half))]


def scatter_pairs(t, rows_axis, cols_axis):
    pairs = []
    for r in range(cols_axis):
        h, target = divmod(r, rows_axis)
        pairs.append((r, target * cols_axis + h * rows_axis + (target ^ t)))
    return pairs


def ring_shifts(cols_axis):
    shifts = [0]
    last = cols_axis // 2 - 1
    for step in range(1, last):
        shifts += [-step, step]
    return shifts + [-last, last, cols_axis // 2]


def place_table(rows_axis, cols_axis, balanced, row_blocks):
    ring = ring_positions(cols_axis)
    groups = cols_axis // rows_axis
    table = []
    for p in range(rows_axis):
        for q in range(cols_axis):
            if balanced:
                places = []
                for shift in ring_shifts(cols_axis):
                    source = ring[(ring.index(q) + shift) % cols_axis]
                    places.append(groups * ((source % rows_axis) ^ p) + source // rows_axis)
            else:
                places = list(range(row_blocks))
            table.append([p, q] + places)
    return np.array(table, np.int32)


def from_root(value, axis, source):
    kept = jnp.where(lax.axis_index(axis) == source, value, 0).astype(value.dtype)
    return lax.psum(kept, axis)


def tie(*values):
    return lax.optimization_barrier(values)


def on_device(matrix):
    rows_axis = lax.axis_size("row")
    cols_axis = lax.axis_size("col")
    both = ("row", "col")
    index = lax.axis_index("row") * cols_axis + lax.axis_index("col")
    row_blocks = matrix.shape[0] // NB
    col_blocks = matrix.shape[1] // NB
    balanced = row_blocks == cols_axis and col_blocks == rows_axis
    table = jnp.asarray(place_table(rows_axis, cols_axis, balanced, row_blocks))
    places = lax.dynamic_slice_in_dim(table, index, 1, 0)[0]

    parts = list(pack_corner(matrix))
    stages = [tree_stages(order) for order in corner_orders(rows_axis, cols_axis)]
    *blocks, head = turn_blocks(matrix, col_blocks)
    first_bit, *other_bits = bits_of(rows_axis)[::-1]
    far = None
    for step in range(len(stages[0])):
        if step == len(stages[0]) - 1 and balanced and False:
            parts[0], parts[1], far = tie(*parts, far)
        came = [lax.ppermute(parts[n], both, stages[n][step][0]) for n in range(2)]
        for n in range(2):
            _, bit, done = stages[n][step]
            parts[n] = jnp.where((index & ~done) == bit, came[n], parts[n])
        if step == 0:
            parts[0], parts[1], head, *blocks = tie(*parts, head, *blocks)
        if step == 0 and balanced:
            _, far = spread_apart([(0, head)], "row", first_bit)[1]
        if step == len(stages[0]) - 2 and balanced:
            parts[0], parts[1], *blocks = tie(*parts, *blocks)
            pieces = [
                lax.ppermute(blocks[t], both, scatter_pairs(t, rows_axis, cols_axis))
                for t in reversed(range(col_blocks))
            ]

    if balanced:
        ring = ring_positions(cols_axis)
        up = [(ring[n], ring[(n + 1) % cols_axis]) for n in range(cols_axis)]
        down = [(b, a) for a, b in up]

        def advance(going, coming):
            return lax.ppermute(going, "col", up), lax.ppermute(coming, "col", down)

        own = [(0, head)]
        for bit in other_bits:
            own = spread_apart(own, "row", bit)
        work, inv_t = factor_first(*parts)
        work, far, *pieces = tie(work, far, *pieces)
        far = [(first_bit, far)]
        for bit in other_bits:
            far = spread_apart(far, "row", bit)
        held = own + far
        chunk = functools.reduce(jnp.add, pieces)
        chunks = [[chunk]]
        going, coming = advance(chunk, chunk)
        work, chunk = tie(work, chunk)
        factor, inv, inv_t = factor_last(work, inv_t)
        inv, going, coming = tie(inv, going, coming)
        chunks.append([going, coming])
        going, coming = advance(going, coming)
    else:
        column = from_root(matrix[:, :NB], "col", 0)
        chunks = [[column[s * NB : (s + 1) * NB] for s in range(row_blocks)]]
        factor, inv, inv_t = factor_last(*factor_first(*parts))
        held = [(0, head)]
        for bit in [first_bit, *other_bits]:
            held = spread_apart(held, "row", bit)

    sources = [matrix] + [v for _, v in sorted(held, key=lambda entry: entry[0])][1:]
    place = len(chunks[0])
    out, across = update(places, 0, chunks[0], factor, inv, inv_t, matrix, sources, None)

    def more(out, part, place):
        return update(places, place, part, factor, inv, inv_t, matrix, [across], out)[0]

    if balanced:
        waiting = chunks[1]
        for step in range(2, cols_axis // 2):
            out, going, coming = tie(out, going, coming)
            waiting = waiting + [going, coming]
            if step < cols_axis // 2 - 1:
                going, coming = advance(going, coming)
            else:
                top = lax.ppermute(going[: NB // 2], "col", up)
                bottom = lax.ppermute(coming[NB // 2 :], "col", down)
            out = more(out, waiting, place)
            place += len(waiting)
            waiting = []
        out = more(out, [jnp.concatenate([top, bottom], 0)], place)
    return out


def solution(mesh):
    in_specs = (P("row", "col"),)
    out_specs = P("row", "col")
    return jax.shard_map(
        on_device, mesh=mesh, in_specs=in_specs, out_specs=out_specs, check_vma=False
    )
```

```python
import functools

import jax
import jax.numpy as jnp
import numpy as np
from jax import lax
from jax.experimental import pallas as pl
from jax.experimental.pallas import tpu as pltpu
from jax.sharding import PartitionSpec as P

NB = 512
SUB = 128
LANES = 8
COUNT = NB // SUB
VMEM_BYTES = 60 * 1024 * 1024
LOWER = [(i, j) for i in range(COUNT) for j in range(i + 1)]
HALF = len(LOWER) // 2
EXACT = lax.Precision.HIGHEST
PARAMS = pltpu.CompilerParams(vmem_limit_bytes=VMEM_BYTES)
SQUARE = jax.ShapeDtypeStruct((NB, NB), jnp.float32)
IN_VMEM = pl.BlockSpec(memory_space=pltpu.VMEM)
ANYWHERE = pl.BlockSpec(memory_space=pl.ANY)


def dot_nt(a, b):
    return lax.dot_general(
        a, b, (((1,), (1,)), ((), ())), precision=EXACT, preferred_element_type=jnp.float32
    )


def dot_nn(a, b):
    return lax.dot_general(
        a, b, (((1,), (0,)), ((), ())), precision=EXACT, preferred_element_type=jnp.float32
    )


def split2(value):
    high = value.astype(jnp.bfloat16)
    low = (value - high.astype(jnp.float32)).astype(jnp.bfloat16)
    return high, low


def split3(value):
    high = value.astype(jnp.bfloat16)
    rest = value - high.astype(jnp.float32)
    middle, low = split2(rest)
    return high, middle, low


def store_parts(ref, value, axis, pattern):
    parts = split3(value)
    half = NB // 2
    for h in range(2):
        for n, k in enumerate(pattern):
            begin = (h * len(pattern) + n) * half
            if axis:
                ref[:, begin : begin + half] = parts[k][:, h * half : (h + 1) * half]
            else:
                ref[begin : begin + half] = parts[k][h * half : (h + 1) * half]


LEFT_PARTS = (0, 1, 2, 0, 1, 0)
RIGHT_PARTS = (0, 0, 0, 1, 1, 2)
DEPTH = len(LEFT_PARTS) * NB


def pack_kernel(matrix_ref, first_ref, second_ref):
    for n, (i, j) in enumerate(LOWER):
        target, place = (first_ref, n) if n < HALF else (second_ref, n - HALF)
        target[place] = matrix_ref[i * SUB : (i + 1) * SUB, j * SUB : (j + 1) * SUB]


def pack_corner(matrix):
    part = jax.ShapeDtypeStruct((HALF, SUB, SUB), jnp.float32)
    whole = pl.BlockSpec((HALF, SUB, SUB), lambda i: (0, 0, 0))
    return pl.pallas_call(
        pack_kernel,
        grid=(1,),
        out_shape=(part, part),
        in_specs=[pl.BlockSpec((NB, NB), lambda i: (0, 0))],
        out_specs=(whole, whole),
        compiler_params=PARAMS,
        name="pack_corner",
    )(matrix)


def turn_kernel(count, matrix_ref, *refs):
    for t in range(count):
        refs[t][...] = matrix_ref[:, t * NB : (t + 1) * NB].T
    refs[count][...] = matrix_ref[...]


def turn_blocks(matrix, count):
    square = pl.BlockSpec((NB, NB), lambda i: (0, 0))
    return pl.pallas_call(
        functools.partial(turn_kernel, count),
        grid=(1,),
        out_shape=(SQUARE,) * count + (jax.ShapeDtypeStruct((NB, count * NB), jnp.float32),),
        in_specs=[pl.BlockSpec((NB, count * NB), lambda i: (0, 0))],
        out_specs=(square,) * count + (pl.BlockSpec((NB, count * NB), lambda i: (0, 0)),),
        compiler_params=PARAMS,
        name="turn_blocks",
    )(matrix)


def reciprocal(value):
    guess = pl.reciprocal(value, approx=True)
    return guess * (2.0 - value * guess)


def small_cholesky(block):
    groups = SUB // LANES
    shape = (LANES, SUB)
    lane = lax.broadcasted_iota(jnp.int32, shape, 1)
    sub = lax.broadcasted_iota(jnp.int32, shape, 0)
    left = [block[g * LANES : (g + 1) * LANES] for g in range(groups)]
    right = [jnp.where(lane == sub + g * LANES, 1.0, 0.0) for g in range(groups)]
    for g0 in range(groups):
        i = g0 * LANES
        head, side = left[g0], right[g0]
        columns = [jnp.broadcast_to(head[:, i + j : i + j + 1], shape) for j in range(LANES)]
        ratios, heads, sides = [], [], []
        for k in range(LANES):
            inverse = reciprocal(columns[k][k : k + 1])
            ratio = {j: columns[j][k : k + 1] * inverse for j in range(k + 1, LANES)}
            scaled_head = head[k : k + 1] * inverse
            scaled_side = side[k : k + 1] * inverse
            ratios.append(ratio)
            heads.append(scaled_head)
            sides.append(scaled_side)
            if k + 1 < LANES:
                below = jnp.where(sub > k, columns[k], 0.0)
                for j in range(k + 1, LANES):
                    columns[j] = columns[j] - below * ratio[j]
                head = head - below * scaled_head
                side = side - below * scaled_side
        left[g0], right[g0] = head, side
        for g in range(g0 + 1, groups):
            own = [jnp.broadcast_to(left[g][:, i + j : i + j + 1], shape) for j in range(LANES)]
            body, tail = left[g], right[g]
            for k in range(LANES):
                for j in range(k + 1, LANES):
                    own[j] = own[j] - own[k] * ratios[k][j]
                body = body - own[k] * heads[k]
                tail = tail - own[k] * sides[k]
            left[g], right[g] = body, tail
    upper, inverse = [], []
    for g in range(groups):
        row = sub + g * LANES
        pivot = jnp.sum(jnp.where(lane == row, left[g], 0.0), axis=1, keepdims=True)
        scale = lax.rsqrt(pivot)
        upper.append(jnp.where(lane >= row, left[g] * scale, 0.0))
        inverse.append(jnp.where(lane <= row, right[g] * scale, 0.0))
    return jnp.concatenate(upper, 0), jnp.concatenate(inverse, 0)


def factor_block(k, work, inv_t):
    start = pl.multiple_of(k * SUB, SUB)
    here = pl.ds(start, SUB)
    upper, inverse = small_cholesky(work[here, here])
    inverse_t = inverse.T
    row = lax.broadcasted_iota(jnp.int32, (NB, SUB), 0)
    panel = jnp.where(row >= start + SUB, dot_nn(work[:, here], inverse_t), 0.0)
    work[...] -= dot_nt(panel, panel)
    work[:, here] = panel
    work[here, here] = upper.T
    column = lax.broadcasted_iota(jnp.int32, (SUB, NB), 1)
    before = jnp.where(column < start, work[here, :], 0.0)
    inv_t[:, here] = -dot_nn(dot_nt(inv_t[...], before), inverse_t)
    inv_t[here, here] = inverse_t


def factor_first_kernel(last, first_ref, second_ref, work, inv_t):
    inv_t[...] = jnp.zeros_like(inv_t)
    work[...] = jnp.zeros_like(work)
    for n, (i, j) in enumerate(LOWER):
        value = first_ref[n] if n < HALF else second_ref[n - HALF]
        work[i * SUB : (i + 1) * SUB, j * SUB : (j + 1) * SUB] = value

    @pl.loop(0, last)
    def _(k):
        factor_block(k, work, inv_t)


def factor_last_kernel(begin, work_in, inv_t_in, factor_ref, inv_ref, inv_t_ref):
    factor_ref[...] = work_in[...]
    inv_t_ref[...] = inv_t_in[...]

    @pl.loop(begin, COUNT)
    def _(k):
        factor_block(k, factor_ref, inv_t_ref)

    inv_ref[...] = inv_t_ref[...].T


FACTOR_COST = pl.CostEstimate(flops=2 * NB**3, bytes_accessed=4 * NB * NB * 4, transcendentals=0)


def factor_first(first, second):
    return pl.pallas_call(
        functools.partial(factor_first_kernel, COUNT // 2),
        out_shape=(SQUARE, SQUARE),
        in_specs=[IN_VMEM] * 2,
        out_specs=(IN_VMEM,) * 2,
        compiler_params=PARAMS,
        cost_estimate=FACTOR_COST,
        name="factor_first",
    )(first, second)


def factor_last(work, inv_t):
    return pl.pallas_call(
        functools.partial(factor_last_kernel, COUNT // 2),
        out_shape=(SQUARE, SQUARE, SQUARE),
        in_specs=[IN_VMEM] * 2,
        out_specs=(IN_VMEM,) * 3,
        compiler_params=PARAMS,
        cost_estimate=FACTOR_COST,
        name="factor_last",
    )(work, inv_t)


def update_kernel(count, ahead, offset, tile, source_count, info, *refs):
    inv_t_ref, matrix_ref = refs[:2]
    chunks = refs[2 : 2 + count]
    sources = refs[2 + count : 2 + count + source_count]
    if ahead:
        factor_ref, inv_ref = refs[2 + count + source_count : 4 + count + source_count]
    out_ref = refs[-12 - ahead]
    across, rows, arrived, panel, panel3, left, right = refs[-11:-4]
    chunk_sems, row_sems, across_sem, out_sem = refs[-4:]
    i, j = pl.program_id(0), pl.program_id(1)
    tiles = across.shape[1] // tile
    half, deep = NB // 2, DEPTH // 2
    first_row = jnp.logical_and(info[0] == 0, info[2 + offset + jnp.maximum(i - ahead, 0)] == 0)
    first_col = jnp.logical_and(info[1] == 0, j == 0)

    def chunk_copy(n):
        return pltpu.make_async_copy(chunks[n], arrived.at[n], chunk_sems.at[n])

    def row_copy(n, t):
        place = pl.ds(t * tile, tile)
        return pltpu.make_async_copy(
            sources[n].at[pl.ds(0, NB), place], rows.at[:, place], row_sems.at[t]
        )

    @pl.when(jnp.logical_and(i == 0, j == 0))
    def _():
        if ahead:
            for n in range(source_count):

                @pl.when(info[0] == n)
                def _():
                    for t in range(tiles):
                        row_copy(n, t).start()

        for n in range(count):
            chunk_copy(n).start()
        if ahead:
            store_parts(left, inv_ref[...], 1, LEFT_PARTS)
        else:
            pltpu.make_async_copy(sources[0], across, across_sem).start()

    if ahead:

        @pl.when(i == 0)
        def _():
            for t in range(tiles):

                @pl.when(j == t)
                def _():
                    row_copy(0, t).wait()
                    for c in range(t * tile, (t + 1) * tile, NB):
                        store_parts(right, rows[:, c : c + NB], 0, RIGHT_PARTS)
                        for h in range(2):
                            part = slice(h * half, (h + 1) * half)
                            value = jnp.dot(
                                left[part, : (h + 1) * deep],
                                right[: (h + 1) * deep],
                                preferred_element_type=jnp.float32,
                            )
                            high, low = split2(value)
                            across[h * half : (h + 1) * half, c : c + NB] = high
                            across[NB + h * half : NB + (h + 1) * half, c : c + NB] = high
                            across[2 * NB + h * half : 2 * NB + (h + 1) * half, c : c + NB] = low

        handed = pltpu.make_async_copy(across, refs[-12], out_sem)

        @pl.when(jnp.logical_and(i == 1, j == 0))
        def _():
            handed.start()

        @pl.when(jnp.logical_and(i == count, j == tiles - 1))
        def _():
            handed.wait()

    @pl.when(jnp.logical_and(i == ahead, j == 0))
    def _():
        store_parts(right, inv_t_ref[...], 0, RIGHT_PARTS)

    @pl.when(jnp.logical_and(i >= ahead, j == 0))
    def _():
        for n in range(count):

            @pl.when(i == n + ahead)
            def _():
                chunk_copy(n).wait()
                store_parts(left, arrived[n], 1, LEFT_PARTS)

        for h in range(2):
            part = slice(h * half, (h + 1) * half)
            value = jnp.dot(
                left[:, : (h + 1) * deep],
                right[: (h + 1) * deep, part],
                preferred_element_type=jnp.float32,
            )
            panel[:, part] = value
            high, low = split2(value)
            panel3[:, h * half : (h + 1) * half] = high
            panel3[:, NB + h * half : NB + (h + 1) * half] = low
            panel3[:, 2 * NB + h * half : 2 * NB + (h + 1) * half] = high

        if ahead:

            @pl.when(first_row)
            def _():
                panel[...] = factor_ref[...]

    if not ahead:

        @pl.when(jnp.logical_and(i == 0, j == 0))
        def _():
            pltpu.make_async_copy(sources[0], across, across_sem).wait()

    @pl.when(jnp.logical_and(i >= ahead, first_row))
    def _():
        out_ref[...] = jnp.zeros_like(out_ref)

    @pl.when(jnp.logical_and(i >= ahead, jnp.logical_not(first_row)))
    def _():
        columns = pl.ds(pl.multiple_of(j * tile, tile), tile)
        product = jnp.dot(panel3[...], across[:, columns], preferred_element_type=jnp.float32)
        out_ref[...] = matrix_ref[...] - product

    @pl.when(jnp.logical_and(i >= ahead, first_col))
    def _():
        out_ref[:, :NB] = panel[...]


def update(info, offset, chunks, factor, inv, inv_t, matrix, sources, base):
    count = len(chunks)
    ahead = 1 if base is None else 0
    width = matrix.shape[1]
    tile = 2 * NB if width % (2 * NB) == 0 else NB
    whole = lambda i, j, info: (0, 0)

    def moving(i, j, info):
        n = i - ahead
        return info[2 + offset + jnp.maximum(n, 0)], jnp.where(n < 0, 0, j)

    square = pl.BlockSpec((NB, NB), whole)
    block = pl.BlockSpec((NB, tile), moving)
    across = jax.ShapeDtypeStruct((3 * NB, width), jnp.bfloat16)
    in_specs = [square, block] + [ANYWHERE] * (count + len(sources))
    operands = [info, inv_t, matrix, *chunks, *sources]
    out_shape, out_specs, aliases = [jax.ShapeDtypeStruct(matrix.shape, jnp.float32)], [block], {}
    if ahead:
        in_specs += [square] * 2
        operands += [factor, inv]
        out_shape.append(across)
        out_specs.append(ANYWHERE)
    else:
        in_specs.append(ANYWHERE)
        operands.append(base)
        aliases = {len(operands) - 1: 0}
    return pl.pallas_call(
        functools.partial(update_kernel, count, ahead, offset, tile, len(sources)),
        grid_spec=pltpu.PrefetchScalarGridSpec(
            num_scalar_prefetch=1,
            grid=(count + ahead, width // tile),
            in_specs=in_specs,
            out_specs=out_specs,
            scratch_shapes=[
                pltpu.VMEM(across.shape, jnp.bfloat16),
                pltpu.VMEM((NB, width) if ahead else (8, 128), jnp.float32),
                pltpu.VMEM((count, NB, NB), jnp.float32),
                pltpu.VMEM((NB, NB), jnp.float32),
                pltpu.VMEM((NB, 3 * NB), jnp.bfloat16),
                pltpu.VMEM((NB, DEPTH), jnp.bfloat16),
                pltpu.VMEM((DEPTH, NB), jnp.bfloat16),
                pltpu.SemaphoreType.DMA((count,)),
                pltpu.SemaphoreType.DMA((width // tile,)),
                pltpu.SemaphoreType.DMA,
                pltpu.SemaphoreType.DMA,
            ],
        ),
        out_shape=out_shape,
        input_output_aliases=aliases,
        compiler_params=PARAMS,
        cost_estimate=pl.CostEstimate(
            flops=6 * (count + ahead) * NB * NB * (width + 2 * NB),
            bytes_accessed=8 * count * NB * width,
            transcendentals=0,
        ),
        name="update_rows",
    )(*operands)


def tree_stages(order):
    reached, done, stages = [0], 0, []
    for bit in order:
        stages.append(([(n, n | bit) for n in reached], bit, done))
        reached = reached + [n | bit for n in reached]
        done |= bit
    return stages


def bits_of(size):
    return [1 << n for n in range(size.bit_length() - 1)]


def corner_orders(rows_axis, cols_axis):
    low = bits_of(cols_axis)
    high = [cols_axis * bit for bit in bits_of(rows_axis)]
    core, across = high[:1], high[:0:-1]
    near, far = low[:1], low[:0:-1]
    return across + near + far + core, across + far + near + core


def spread_apart(held, axis, bit):
    return held + [(n | bit, lax.ppermute(v, axis, [(n, n | bit)])) for n, v in held]


def ring_positions(cols_axis):
    half = cols_axis // 2
    return [2 * n for n in range(half)] + [2 * n + 1 for n in reversed(range(half))]


def scatter_pairs(t, rows_axis, cols_axis):
    pairs = []
    for r in range(cols_axis):
        h, target = divmod(r, rows_axis)
        pairs.append((r, target * cols_axis + h * rows_axis + (target ^ t)))
    return [(a, b) for a, b in pairs if a != b]


def ring_shifts(cols_axis):
    shifts = [0]
    last = cols_axis // 2 - 1
    for step in range(1, last):
        shifts += [-step, step]
    return shifts + [-last, last, cols_axis // 2]


def place_table(rows_axis, cols_axis, balanced, row_blocks):
    ring = ring_positions(cols_axis)
    groups = cols_axis // rows_axis
    table = []
    for p in range(rows_axis):
        for q in range(cols_axis):
            if balanced:
                places = []
                for shift in ring_shifts(cols_axis):
                    source = ring[(ring.index(q) + shift) % cols_axis]
                    places.append(groups * ((source % rows_axis) ^ p) + source // rows_axis)
            else:
                places = list(range(row_blocks))
            table.append([p, q] + places)
    return np.array(table, np.int32)


def from_root(value, axis, source):
    kept = jnp.where(lax.axis_index(axis) == source, value, 0).astype(value.dtype)
    return lax.psum(kept, axis)


def tie(*values):
    return lax.optimization_barrier(values)


def on_device(matrix):
    rows_axis = lax.axis_size("row")
    cols_axis = lax.axis_size("col")
    both = ("row", "col")
    index = lax.axis_index("row") * cols_axis + lax.axis_index("col")
    row_blocks = matrix.shape[0] // NB
    col_blocks = matrix.shape[1] // NB
    balanced = row_blocks == cols_axis and col_blocks == rows_axis
    table = jnp.asarray(place_table(rows_axis, cols_axis, balanced, row_blocks))
    places = lax.dynamic_slice_in_dim(table, index, 1, 0)[0]

    parts = list(pack_corner(matrix))
    stages = [tree_stages(order) for order in corner_orders(rows_axis, cols_axis)]
    *blocks, head = turn_blocks(matrix, col_blocks)
    first_bit, *other_bits = bits_of(rows_axis)[::-1]
    far = None
    for step in range(len(stages[0])):
        if step == len(stages[0]) - 1 and balanced and False:
            parts[0], parts[1], far = tie(*parts, far)
        came = [lax.ppermute(parts[n], both, stages[n][step][0]) for n in range(2)]
        for n in range(2):
            _, bit, done = stages[n][step]
            parts[n] = jnp.where((index & ~done) == bit, came[n], parts[n])
        if step == 0:
            parts[0], parts[1], head, *blocks = tie(*parts, head, *blocks)
        if step == 0 and balanced:
            _, far = spread_apart([(0, head)], "row", first_bit)[1]
        if step == len(stages[0]) - 2 and balanced:
            parts[0], parts[1], *blocks = tie(*parts, *blocks)
            pieces = [
                lax.ppermute(blocks[t], both, scatter_pairs(t, rows_axis, cols_axis))
                for t in reversed(range(col_blocks))
            ]

    if balanced:
        ring = ring_positions(cols_axis)
        up = [(ring[n], ring[(n + 1) % cols_axis]) for n in range(cols_axis)]
        down = [(b, a) for a, b in up]

        def advance(going, coming):
            return lax.ppermute(going, "col", up), lax.ppermute(coming, "col", down)

        own = [(0, head)]
        for bit in other_bits:
            own = spread_apart(own, "row", bit)
        work, inv_t = factor_first(*parts)
        work, far, *pieces = tie(work, far, *pieces)
        far = [(first_bit, far)]
        for bit in other_bits:
            far = spread_apart(far, "row", bit)
        held = own + far
        own_block = jnp.logical_and(index < cols_axis, index % rows_axis == 0)
        chunk = jnp.where(own_block, blocks[0], functools.reduce(jnp.add, pieces))
        chunks = [[chunk]]
        going, coming = advance(chunk, chunk)
        work, chunk = tie(work, chunk)
        factor, inv, inv_t = factor_last(work, inv_t)
        inv, going, coming = tie(inv, going, coming)
        chunks.append([going, coming])
        going, coming = advance(going, coming)
    else:
        column = from_root(matrix[:, :NB], "col", 0)
        chunks = [[column[s * NB : (s + 1) * NB] for s in range(row_blocks)]]
        factor, inv, inv_t = factor_last(*factor_first(*parts))
        held = [(0, head)]
        for bit in [first_bit, *other_bits]:
            held = spread_apart(held, "row", bit)

    sources = [matrix] + [v for _, v in sorted(held, key=lambda entry: entry[0])][1:]
    place = len(chunks[0])
    out, across = update(places, 0, chunks[0], factor, inv, inv_t, matrix, sources, None)

    def more(out, part, place):
        return update(places, place, part, factor, inv, inv_t, matrix, [across], out)[0]

    if balanced:
        waiting = chunks[1]
        for step in range(2, cols_axis // 2):
            out, going, coming = tie(out, going, coming)
            waiting = waiting + [going, coming]
            if step < cols_axis // 2 - 1:
                going, coming = advance(going, coming)
            else:
                top = lax.ppermute(going[: NB // 2], "col", up)
                bottom = lax.ppermute(coming[NB // 2 :], "col", down)
            out = more(out, waiting, place)
            place += len(waiting)
            waiting = []
        out = more(out, [jnp.concatenate([top, bottom], 0)], place)
    return out


def solution(mesh):
    in_specs = (P("row", "col"),)
    out_specs = P("row", "col")
    return jax.shard_map(
        on_device, mesh=mesh, in_specs=in_specs, out_specs=out_specs, check_vma=False
    )
```

```python
import functools

import jax
import jax.numpy as jnp
import numpy as np
from jax import lax
from jax.experimental import pallas as pl
from jax.experimental.pallas import tpu as pltpu
from jax.sharding import PartitionSpec as P

NB = 512
SUB = 128
LANES = 8
COUNT = NB // SUB
VMEM_BYTES = 60 * 1024 * 1024
LOWER = [(i, j) for i in range(COUNT) for j in range(i + 1)]
HALF = len(LOWER) // 2
EXACT = lax.Precision.HIGHEST
PARAMS = pltpu.CompilerParams(vmem_limit_bytes=VMEM_BYTES)
SQUARE = jax.ShapeDtypeStruct((NB, NB), jnp.float32)
IN_VMEM = pl.BlockSpec(memory_space=pltpu.VMEM)
ANYWHERE = pl.BlockSpec(memory_space=pl.ANY)


def dot_nt(a, b):
    return lax.dot_general(
        a, b, (((1,), (1,)), ((), ())), precision=EXACT, preferred_element_type=jnp.float32
    )


def dot_nn(a, b):
    return lax.dot_general(
        a, b, (((1,), (0,)), ((), ())), precision=EXACT, preferred_element_type=jnp.float32
    )


def split2(value):
    high = value.astype(jnp.bfloat16)
    low = (value - high.astype(jnp.float32)).astype(jnp.bfloat16)
    return high, low


def split3(value):
    high = value.astype(jnp.bfloat16)
    rest = value - high.astype(jnp.float32)
    middle, low = split2(rest)
    return high, middle, low


def store_parts(ref, value, axis, pattern):
    parts = split3(value)
    half = NB // 2
    for h in range(2):
        for n, k in enumerate(pattern):
            begin = (h * len(pattern) + n) * half
            if axis:
                ref[:, begin : begin + half] = parts[k][:, h * half : (h + 1) * half]
            else:
                ref[begin : begin + half] = parts[k][h * half : (h + 1) * half]


LEFT_PARTS = (0, 1, 2, 0, 1, 0)
RIGHT_PARTS = (0, 0, 0, 1, 1, 2)
DEPTH = len(LEFT_PARTS) * NB


def pack_kernel(matrix_ref, first_ref, second_ref):
    for n, (i, j) in enumerate(LOWER):
        target, place = (first_ref, n) if n < HALF else (second_ref, n - HALF)
        target[place] = matrix_ref[i * SUB : (i + 1) * SUB, j * SUB : (j + 1) * SUB]


def pack_corner(matrix):
    part = jax.ShapeDtypeStruct((HALF, SUB, SUB), jnp.float32)
    whole = pl.BlockSpec((HALF, SUB, SUB), lambda i: (0, 0, 0))
    return pl.pallas_call(
        pack_kernel,
        grid=(1,),
        out_shape=(part, part),
        in_specs=[pl.BlockSpec((NB, NB), lambda i: (0, 0))],
        out_specs=(whole, whole),
        compiler_params=PARAMS,
        name="pack_corner",
    )(matrix)


def turn_kernel(count, matrix_ref, *refs):
    for t in range(count):
        refs[t][...] = matrix_ref[:, t * NB : (t + 1) * NB].T
    refs[count][...] = matrix_ref[...]


def turn_blocks(matrix, count):
    square = pl.BlockSpec((NB, NB), lambda i: (0, 0))
    return pl.pallas_call(
        functools.partial(turn_kernel, count),
        grid=(1,),
        out_shape=(SQUARE,) * count + (jax.ShapeDtypeStruct((NB, count * NB), jnp.float32),),
        in_specs=[pl.BlockSpec((NB, count * NB), lambda i: (0, 0))],
        out_specs=(square,) * count + (pl.BlockSpec((NB, count * NB), lambda i: (0, 0)),),
        compiler_params=PARAMS,
        name="turn_blocks",
    )(matrix)


def reciprocal(value):
    guess = pl.reciprocal(value, approx=True)
    return guess * (2.0 - value * guess)


def small_cholesky(block):
    groups = SUB // LANES
    shape = (LANES, SUB)
    lane = lax.broadcasted_iota(jnp.int32, shape, 1)
    sub = lax.broadcasted_iota(jnp.int32, shape, 0)
    left = [block[g * LANES : (g + 1) * LANES] for g in range(groups)]
    right = [jnp.where(lane == sub + g * LANES, 1.0, 0.0) for g in range(groups)]
    for g0 in range(groups):
        i = g0 * LANES
        head, side = left[g0], right[g0]
        columns = [jnp.broadcast_to(head[:, i + j : i + j + 1], shape) for j in range(LANES)]
        ratios, heads, sides = [], [], []
        for k in range(LANES):
            inverse = reciprocal(columns[k][k : k + 1])
            ratio = {j: columns[j][k : k + 1] * inverse for j in range(k + 1, LANES)}
            scaled_head = head[k : k + 1] * inverse
            scaled_side = side[k : k + 1] * inverse
            ratios.append(ratio)
            heads.append(scaled_head)
            sides.append(scaled_side)
            if k + 1 < LANES:
                below = jnp.where(sub > k, columns[k], 0.0)
                for j in range(k + 1, LANES):
                    columns[j] = columns[j] - below * ratio[j]
                head = head - below * scaled_head
                side = side - below * scaled_side
        left[g0], right[g0] = head, side
        for g in range(g0 + 1, groups):
            own = [jnp.broadcast_to(left[g][:, i + j : i + j + 1], shape) for j in range(LANES)]
            body, tail = left[g], right[g]
            for k in range(LANES):
                for j in range(k + 1, LANES):
                    own[j] = own[j] - own[k] * ratios[k][j]
                body = body - own[k] * heads[k]
                tail = tail - own[k] * sides[k]
            left[g], right[g] = body, tail
    upper, inverse = [], []
    for g in range(groups):
        row = sub + g * LANES
        pivot = jnp.sum(jnp.where(lane == row, left[g], 0.0), axis=1, keepdims=True)
        scale = lax.rsqrt(pivot)
        upper.append(jnp.where(lane >= row, left[g] * scale, 0.0))
        inverse.append(jnp.where(lane <= row, right[g] * scale, 0.0))
    return jnp.concatenate(upper, 0), jnp.concatenate(inverse, 0)


def factor_block(k, work, inv_t):
    start = pl.multiple_of(k * SUB, SUB)
    here = pl.ds(start, SUB)
    upper, inverse = small_cholesky(work[here, here])
    inverse_t = inverse.T
    row = lax.broadcasted_iota(jnp.int32, (NB, SUB), 0)
    panel = jnp.where(row >= start + SUB, dot_nn(work[:, here], inverse_t), 0.0)
    work[...] -= dot_nt(panel, panel)
    work[:, here] = panel
    work[here, here] = upper.T
    column = lax.broadcasted_iota(jnp.int32, (SUB, NB), 1)
    before = jnp.where(column < start, work[here, :], 0.0)
    inv_t[:, here] = -dot_nn(dot_nt(inv_t[...], before), inverse_t)
    inv_t[here, here] = inverse_t


def factor_first_kernel(last, first_ref, second_ref, work, inv_t):
    inv_t[...] = jnp.zeros_like(inv_t)
    work[...] = jnp.zeros_like(work)
    for n, (i, j) in enumerate(LOWER):
        value = first_ref[n] if n < HALF else second_ref[n - HALF]
        work[i * SUB : (i + 1) * SUB, j * SUB : (j + 1) * SUB] = value

    @pl.loop(0, last)
    def _(k):
        factor_block(k, work, inv_t)


def factor_last_kernel(begin, work_in, inv_t_in, factor_ref, inv_ref, inv_t_ref):
    factor_ref[...] = work_in[...]
    inv_t_ref[...] = inv_t_in[...]

    @pl.loop(begin, COUNT)
    def _(k):
        factor_block(k, factor_ref, inv_t_ref)

    inv_ref[...] = inv_t_ref[...].T


FACTOR_COST = pl.CostEstimate(flops=2 * NB**3, bytes_accessed=4 * NB * NB * 4, transcendentals=0)


def factor_first(first, second):
    return pl.pallas_call(
        functools.partial(factor_first_kernel, COUNT - 1),
        out_shape=(SQUARE, SQUARE),
        in_specs=[IN_VMEM] * 2,
        out_specs=(IN_VMEM,) * 2,
        compiler_params=PARAMS,
        cost_estimate=FACTOR_COST,
        name="factor_first",
    )(first, second)


def factor_last(work, inv_t):
    return pl.pallas_call(
        functools.partial(factor_last_kernel, COUNT - 1),
        out_shape=(SQUARE, SQUARE, SQUARE),
        in_specs=[IN_VMEM] * 2,
        out_specs=(IN_VMEM,) * 3,
        compiler_params=PARAMS,
        cost_estimate=FACTOR_COST,
        name="factor_last",
    )(work, inv_t)


def update_kernel(spans, ahead, offset, tile, source_count, info, *refs):
    count = spans[-1][0] + 1
    inv_t_ref, matrix_ref = refs[:2]
    begin = 2 + len(spans)
    chunks = refs[2:begin]
    sources = refs[begin : begin + source_count]
    if ahead:
        factor_ref, inv_ref = refs[begin + source_count : begin + source_count + 2]
    out_ref = refs[-12 - ahead]
    across, rows, arrived, panel, panel3, left, right = refs[-11:-4]
    chunk_sems, row_sems, across_sem, out_sem = refs[-4:]
    i, j = pl.program_id(0), pl.program_id(1)
    tiles = across.shape[1] // tile
    half, deep = NB // 2, DEPTH // 2
    first_row = jnp.logical_and(info[0] == 0, info[2 + offset + jnp.maximum(i - ahead, 0)] == 0)
    first_col = jnp.logical_and(info[1] == 0, j == 0)

    def chunk_copy(k):
        n, first, size = spans[k]
        return pltpu.make_async_copy(chunks[k], arrived.at[n, pl.ds(first, size)], chunk_sems.at[k])

    def row_copy(n, t):
        place = pl.ds(t * tile, tile)
        return pltpu.make_async_copy(
            sources[n].at[pl.ds(0, NB), place], rows.at[:, place], row_sems.at[t]
        )

    @pl.when(jnp.logical_and(i == 0, j == 0))
    def _():
        if ahead:
            for n in range(source_count):

                @pl.when(info[0] == n)
                def _():
                    for t in range(tiles):
                        row_copy(n, t).start()

        for k in range(len(spans)):
            chunk_copy(k).start()
        if ahead:
            store_parts(left, inv_ref[...], 1, LEFT_PARTS)
        else:
            pltpu.make_async_copy(sources[0], across, across_sem).start()

    if ahead:

        @pl.when(i == 0)
        def _():
            for t in range(tiles):

                @pl.when(j == t)
                def _():
                    row_copy(0, t).wait()
                    for c in range(t * tile, (t + 1) * tile, NB):
                        store_parts(right, rows[:, c : c + NB], 0, RIGHT_PARTS)
                        for h in range(2):
                            part = slice(h * half, (h + 1) * half)
                            value = jnp.dot(
                                left[part, : (h + 1) * deep],
                                right[: (h + 1) * deep],
                                preferred_element_type=jnp.float32,
                            )
                            high, low = split2(value)
                            across[h * half : (h + 1) * half, c : c + NB] = high
                            across[NB + h * half : NB + (h + 1) * half, c : c + NB] = high
                            across[2 * NB + h * half : 2 * NB + (h + 1) * half, c : c + NB] = low

        handed = pltpu.make_async_copy(across, refs[-12], out_sem)

        @pl.when(jnp.logical_and(i == 1, j == 0))
        def _():
            handed.start()

        @pl.when(jnp.logical_and(i == count, j == tiles - 1))
        def _():
            handed.wait()

    @pl.when(jnp.logical_and(i == ahead, j == 0))
    def _():
        store_parts(right, inv_t_ref[...], 0, RIGHT_PARTS)

    @pl.when(jnp.logical_and(i >= ahead, j == 0))
    def _():
        for n in range(count):

            @pl.when(i == n + ahead)
            def _():
                for k in range(len(spans)):
                    if spans[k][0] == n:
                        chunk_copy(k).wait()
                store_parts(left, arrived[n], 1, LEFT_PARTS)

        for h in range(2):
            part = slice(h * half, (h + 1) * half)
            value = jnp.dot(
                left[:, : (h + 1) * deep],
                right[: (h + 1) * deep, part],
                preferred_element_type=jnp.float32,
            )
            panel[:, part] = value
            high, low = split2(value)
            panel3[:, h * half : (h + 1) * half] = high
            panel3[:, NB + h * half : NB + (h + 1) * half] = low
            panel3[:, 2 * NB + h * half : 2 * NB + (h + 1) * half] = high

        if ahead:

            @pl.when(first_row)
            def _():
                panel[...] = factor_ref[...]

    if not ahead:

        @pl.when(jnp.logical_and(i == 0, j == 0))
        def _():
            pltpu.make_async_copy(sources[0], across, across_sem).wait()

    @pl.when(jnp.logical_and(i >= ahead, first_row))
    def _():
        out_ref[...] = jnp.zeros_like(out_ref)

    @pl.when(jnp.logical_and(i >= ahead, jnp.logical_not(first_row)))
    def _():
        columns = pl.ds(pl.multiple_of(j * tile, tile), tile)
        product = jnp.dot(panel3[...], across[:, columns], preferred_element_type=jnp.float32)
        out_ref[...] = matrix_ref[...] - product

    @pl.when(jnp.logical_and(i >= ahead, first_col))
    def _():
        out_ref[:, :NB] = panel[...]


def update(info, offset, chunks, factor, inv, inv_t, matrix, sources, base):
    count = len(chunks)
    pieces, spans = [], []
    for n, chunk in enumerate(chunks):
        first = 0
        for piece in chunk if isinstance(chunk, tuple) else (chunk,):
            pieces.append(piece)
            spans.append((n, first, piece.shape[0]))
            first += piece.shape[0]
    ahead = 1 if base is None else 0
    width = matrix.shape[1]
    tile = 2 * NB if width % (2 * NB) == 0 else NB
    whole = lambda i, j, info: (0, 0)

    def moving(i, j, info):
        n = i - ahead
        return info[2 + offset + jnp.maximum(n, 0)], jnp.where(n < 0, 0, j)

    square = pl.BlockSpec((NB, NB), whole)
    block = pl.BlockSpec((NB, tile), moving)
    across = jax.ShapeDtypeStruct((3 * NB, width), jnp.bfloat16)
    in_specs = [square, block] + [ANYWHERE] * (len(pieces) + len(sources))
    operands = [info, inv_t, matrix, *pieces, *sources]
    out_shape, out_specs, aliases = [jax.ShapeDtypeStruct(matrix.shape, jnp.float32)], [block], {}
    if ahead:
        in_specs += [square] * 2
        operands += [factor, inv]
        out_shape.append(across)
        out_specs.append(ANYWHERE)
    else:
        in_specs.append(ANYWHERE)
        operands.append(base)
        aliases = {len(operands) - 1: 0}
    return pl.pallas_call(
        functools.partial(update_kernel, spans, ahead, offset, tile, len(sources)),
        grid_spec=pltpu.PrefetchScalarGridSpec(
            num_scalar_prefetch=1,
            grid=(count + ahead, width // tile),
            in_specs=in_specs,
            out_specs=out_specs,
            scratch_shapes=[
                pltpu.VMEM(across.shape, jnp.bfloat16),
                pltpu.VMEM((NB, width) if ahead else (8, 128), jnp.float32),
                pltpu.VMEM((count, NB, NB), jnp.float32),
                pltpu.VMEM((NB, NB), jnp.float32),
                pltpu.VMEM((NB, 3 * NB), jnp.bfloat16),
                pltpu.VMEM((NB, DEPTH), jnp.bfloat16),
                pltpu.VMEM((DEPTH, NB), jnp.bfloat16),
                pltpu.SemaphoreType.DMA((len(pieces),)),
                pltpu.SemaphoreType.DMA((width // tile,)),
                pltpu.SemaphoreType.DMA,
                pltpu.SemaphoreType.DMA,
            ],
        ),
        out_shape=out_shape,
        input_output_aliases=aliases,
        compiler_params=PARAMS,
        cost_estimate=pl.CostEstimate(
            flops=6 * (count + ahead) * NB * NB * (width + 2 * NB),
            bytes_accessed=8 * count * NB * width,
            transcendentals=0,
        ),
        name="update_rows",
    )(*operands)


def tree_stages(order):
    reached, done, stages = [0], 0, []
    for bit in order:
        stages.append(([(n, n | bit) for n in reached], bit, done))
        reached = reached + [n | bit for n in reached]
        done |= bit
    return stages


def bits_of(size):
    return [1 << n for n in range(size.bit_length() - 1)]


def corner_orders(rows_axis, cols_axis):
    low = bits_of(cols_axis)
    high = [cols_axis * bit for bit in bits_of(rows_axis)]
    core, across = high[:1], high[:0:-1]
    near, far = low[:1], low[:0:-1]
    return across + near + far + core, across + far + near + core


def spread_apart(held, axis, bit):
    return held + [(n | bit, lax.ppermute(v, axis, [(n, n | bit)])) for n, v in held]


def ring_positions(cols_axis):
    half = cols_axis // 2
    return [2 * n for n in range(half)] + [2 * n + 1 for n in reversed(range(half))]


def scatter_pairs(t, rows_axis, cols_axis):
    pairs = []
    for r in range(cols_axis):
        h, target = divmod(r, rows_axis)
        pairs.append((r, target * cols_axis + h * rows_axis + (target ^ t)))
    return [(a, b) for a, b in pairs if a != b]


def ring_shifts(cols_axis):
    shifts = [0]
    last = cols_axis // 2 - 1
    for step in range(1, last):
        shifts += [-step, step]
    return shifts + [-last, last, cols_axis // 2]


def place_table(rows_axis, cols_axis, balanced, row_blocks):
    ring = ring_positions(cols_axis)
    groups = cols_axis // rows_axis
    table = []
    for p in range(rows_axis):
        for q in range(cols_axis):
            if balanced:
                places = []
                for shift in ring_shifts(cols_axis):
                    source = ring[(ring.index(q) + shift) % cols_axis]
                    places.append(groups * ((source % rows_axis) ^ p) + source // rows_axis)
            else:
                places = list(range(row_blocks))
            table.append([p, q] + places)
    return np.array(table, np.int32)


def from_root(value, axis, source):
    kept = jnp.where(lax.axis_index(axis) == source, value, 0).astype(value.dtype)
    return lax.psum(kept, axis)


def tie(*values):
    return lax.optimization_barrier(values)


def on_device(matrix):
    rows_axis = lax.axis_size("row")
    cols_axis = lax.axis_size("col")
    both = ("row", "col")
    index = lax.axis_index("row") * cols_axis + lax.axis_index("col")
    row_blocks = matrix.shape[0] // NB
    col_blocks = matrix.shape[1] // NB
    balanced = row_blocks == cols_axis and col_blocks == rows_axis
    table = jnp.asarray(place_table(rows_axis, cols_axis, balanced, row_blocks))
    places = lax.dynamic_slice_in_dim(table, index, 1, 0)[0]

    parts = list(pack_corner(matrix))
    stages = [tree_stages(order) for order in corner_orders(rows_axis, cols_axis)]
    *blocks, head = turn_blocks(matrix, col_blocks)
    first_bit, *other_bits = bits_of(rows_axis)[::-1]
    far = None
    for step in range(len(stages[0])):
        if step == len(stages[0]) - 1 and balanced and False:
            parts[0], parts[1], far = tie(*parts, far)
        came = [lax.ppermute(parts[n], both, stages[n][step][0]) for n in range(2)]
        for n in range(2):
            _, bit, done = stages[n][step]
            parts[n] = jnp.where((index & ~done) == bit, came[n], parts[n])
        if step == 0:
            parts[0], parts[1], head, *blocks = tie(*parts, head, *blocks)
        if step == 0 and balanced:
            _, far = spread_apart([(0, head)], "row", first_bit)[1]
        if step == len(stages[0]) - 2 and balanced:
            parts[0], parts[1], *blocks = tie(*parts, *blocks)
            pieces = [
                lax.ppermute(blocks[t], both, scatter_pairs(t, rows_axis, cols_axis))
                for t in reversed(range(col_blocks))
            ]

    if balanced:
        ring = ring_positions(cols_axis)
        up = [(ring[n], ring[(n + 1) % cols_axis]) for n in range(cols_axis)]
        down = [(b, a) for a, b in up]

        def advance(going, coming):
            return lax.ppermute(going, "col", up), lax.ppermute(coming, "col", down)

        own = [(0, head)]
        for bit in other_bits:
            own = spread_apart(own, "row", bit)
        work, inv_t = factor_first(*parts)
        work, far, *pieces = tie(work, far, *pieces)
        far = [(first_bit, far)]
        for bit in other_bits:
            far = spread_apart(far, "row", bit)
        held = own + far
        own_block = jnp.logical_and(index < cols_axis, index % rows_axis == 0)
        chunk = jnp.where(own_block, blocks[0], functools.reduce(jnp.add, pieces))
        chunks = [[chunk]]
        going, coming = advance(chunk, chunk)
        work, chunk = tie(work, chunk)
        factor, inv, inv_t = factor_last(work, inv_t)
    else:
        column = from_root(matrix[:, :NB], "col", 0)
        chunks = [[column[s * NB : (s + 1) * NB] for s in range(row_blocks)]]
        factor, inv, inv_t = factor_last(*factor_first(*parts))
        held = [(0, head)]
        for bit in [first_bit, *other_bits]:
            held = spread_apart(held, "row", bit)

    sources = [matrix] + [v for _, v in sorted(held, key=lambda entry: entry[0])][1:]
    place = len(chunks[0])
    out, across = update(places, 0, chunks[0], factor, inv, inv_t, matrix, sources, None)

    def more(out, part, place):
        return update(places, place, part, factor, inv, inv_t, matrix, [across], out)[0]

    if balanced:
        for step in range(1, cols_axis // 2):
            out, going, coming = tie(out, going, coming)
            part = [going, coming]
            if step < cols_axis // 2 - 1:
                going, coming = advance(going, coming)
            else:
                top = lax.ppermute(going[: NB // 2], "col", up)
                bottom = lax.ppermute(coming[NB // 2 :], "col", down)
            out = more(out, part, place)
            place += len(part)
        out = more(out, [(top, bottom)], place)
    return out


def solution(mesh):
    in_specs = (P("row", "col"),)
    out_specs = P("row", "col")
    return jax.shard_map(
        on_device, mesh=mesh, in_specs=in_specs, out_specs=out_specs, check_vma=False
    )
```

```python
import functools

import jax
import jax.numpy as jnp
import numpy as np
from jax import lax
from jax.experimental import pallas as pl
from jax.experimental.pallas import tpu as pltpu
from jax.sharding import PartitionSpec as P

NB = 512
SUB = 128
LANES = 8
COUNT = NB // SUB
VMEM_BYTES = 60 * 1024 * 1024
LOWER = [(i, j) for i in range(COUNT) for j in range(i + 1)]
HALF = len(LOWER) // 2
EXACT = lax.Precision.HIGHEST
PARAMS = pltpu.CompilerParams(vmem_limit_bytes=VMEM_BYTES)
SQUARE = jax.ShapeDtypeStruct((NB, NB), jnp.float32)
IN_VMEM = pl.BlockSpec(memory_space=pltpu.VMEM)
ANYWHERE = pl.BlockSpec(memory_space=pl.ANY)


def dot_nt(a, b):
    return lax.dot_general(
        a, b, (((1,), (1,)), ((), ())), precision=EXACT, preferred_element_type=jnp.float32
    )


def dot_nn(a, b):
    return lax.dot_general(
        a, b, (((1,), (0,)), ((), ())), precision=EXACT, preferred_element_type=jnp.float32
    )


def split2(value):
    high = value.astype(jnp.bfloat16)
    low = (value - high.astype(jnp.float32)).astype(jnp.bfloat16)
    return high, low


def split3(value):
    high = value.astype(jnp.bfloat16)
    rest = value - high.astype(jnp.float32)
    middle, low = split2(rest)
    return high, middle, low


def store_parts(ref, value, axis, pattern):
    parts = split3(value)
    half = NB // 2
    for h in range(2):
        for n, k in enumerate(pattern):
            begin = (h * len(pattern) + n) * half
            if axis:
                ref[:, begin : begin + half] = parts[k][:, h * half : (h + 1) * half]
            else:
                ref[begin : begin + half] = parts[k][h * half : (h + 1) * half]


LEFT_PARTS = (0, 1, 2, 0, 1, 0)
RIGHT_PARTS = (0, 0, 0, 1, 1, 2)
DEPTH = len(LEFT_PARTS) * NB


def pack_kernel(matrix_ref, first_ref, second_ref):
    for n, (i, j) in enumerate(LOWER):
        target, place = (first_ref, n) if n < HALF else (second_ref, n - HALF)
        target[place] = matrix_ref[i * SUB : (i + 1) * SUB, j * SUB : (j + 1) * SUB]


def pack_corner(matrix):
    part = jax.ShapeDtypeStruct((HALF, SUB, SUB), jnp.float32)
    whole = pl.BlockSpec((HALF, SUB, SUB), lambda i: (0, 0, 0))
    return pl.pallas_call(
        pack_kernel,
        grid=(1,),
        out_shape=(part, part),
        in_specs=[pl.BlockSpec((NB, NB), lambda i: (0, 0))],
        out_specs=(whole, whole),
        compiler_params=PARAMS,
        name="pack_corner",
    )(matrix)


def turn_kernel(count, matrix_ref, *refs):
    for t in range(count):
        refs[t][...] = matrix_ref[:, t * NB : (t + 1) * NB].T
    refs[count][...] = matrix_ref[...]


def turn_blocks(matrix, count):
    square = pl.BlockSpec((NB, NB), lambda i: (0, 0))
    return pl.pallas_call(
        functools.partial(turn_kernel, count),
        grid=(1,),
        out_shape=(SQUARE,) * count + (jax.ShapeDtypeStruct((NB, count * NB), jnp.float32),),
        in_specs=[pl.BlockSpec((NB, count * NB), lambda i: (0, 0))],
        out_specs=(square,) * count + (pl.BlockSpec((NB, count * NB), lambda i: (0, 0)),),
        compiler_params=PARAMS,
        name="turn_blocks",
    )(matrix)


def reciprocal(value):
    return pl.reciprocal(value, approx=True)


def small_cholesky(block):
    groups = SUB // LANES
    shape = (LANES, SUB)
    lane = lax.broadcasted_iota(jnp.int32, shape, 1)
    sub = lax.broadcasted_iota(jnp.int32, shape, 0)
    left = [block[g * LANES : (g + 1) * LANES] for g in range(groups)]
    right = [jnp.where(lane == sub + g * LANES, 1.0, 0.0) for g in range(groups)]
    for g0 in range(groups):
        i = g0 * LANES
        head, side = left[g0], right[g0]
        columns = [jnp.broadcast_to(head[:, i + j : i + j + 1], shape) for j in range(LANES)]
        ratios, heads, sides = [], [], []
        for k in range(LANES):
            inverse = reciprocal(columns[k][k : k + 1])
            ratio = {j: columns[j][k : k + 1] * inverse for j in range(k + 1, LANES)}
            scaled_head = head[k : k + 1] * inverse
            scaled_side = side[k : k + 1] * inverse
            ratios.append(ratio)
            heads.append(scaled_head)
            sides.append(scaled_side)
            if k + 1 < LANES:
                below = jnp.where(sub > k, columns[k], 0.0)
                for j in range(k + 1, LANES):
                    columns[j] = columns[j] - below * ratio[j]
                head = head - below * scaled_head
                side = side - below * scaled_side
        left[g0], right[g0] = head, side
        for g in range(g0 + 1, groups):
            own = [jnp.broadcast_to(left[g][:, i + j : i + j + 1], shape) for j in range(LANES)]
            body, tail = left[g], right[g]
            for k in range(LANES):
                for j in range(k + 1, LANES):
                    own[j] = own[j] - own[k] * ratios[k][j]
                body = body - own[k] * heads[k]
                tail = tail - own[k] * sides[k]
            left[g], right[g] = body, tail
    upper, inverse = [], []
    for g in range(groups):
        row = sub + g * LANES
        pivot = jnp.sum(jnp.where(lane == row, left[g], 0.0), axis=1, keepdims=True)
        scale = lax.rsqrt(pivot)
        upper.append(jnp.where(lane >= row, left[g] * scale, 0.0))
        inverse.append(jnp.where(lane <= row, right[g] * scale, 0.0))
    return jnp.concatenate(upper, 0), jnp.concatenate(inverse, 0)


def factor_block(k, work, inv_t):
    start = pl.multiple_of(k * SUB, SUB)
    here = pl.ds(start, SUB)
    upper, inverse = small_cholesky(work[here, here])
    inverse_t = inverse.T
    row = lax.broadcasted_iota(jnp.int32, (NB, SUB), 0)
    panel = jnp.where(row >= start + SUB, dot_nn(work[:, here], inverse_t), 0.0)
    work[...] -= dot_nt(panel, panel)
    work[:, here] = panel
    work[here, here] = upper.T
    column = lax.broadcasted_iota(jnp.int32, (SUB, NB), 1)
    before = jnp.where(column < start, work[here, :], 0.0)
    inv_t[:, here] = -dot_nn(dot_nt(inv_t[...], before), inverse_t)
    inv_t[here, here] = inverse_t


def factor_first_kernel(last, first_ref, second_ref, work, inv_t):
    inv_t[...] = jnp.zeros_like(inv_t)
    work[...] = jnp.zeros_like(work)
    for n, (i, j) in enumerate(LOWER):
        value = first_ref[n] if n < HALF else second_ref[n - HALF]
        work[i * SUB : (i + 1) * SUB, j * SUB : (j + 1) * SUB] = value

    @pl.loop(0, last)
    def _(k):
        factor_block(k, work, inv_t)


def factor_last_kernel(begin, work_in, inv_t_in, factor_ref, inv_ref, inv_t_ref):
    factor_ref[...] = work_in[...]
    inv_t_ref[...] = inv_t_in[...]

    @pl.loop(begin, COUNT)
    def _(k):
        factor_block(k, factor_ref, inv_t_ref)

    inv_ref[...] = inv_t_ref[...].T


FACTOR_COST = pl.CostEstimate(flops=2 * NB**3, bytes_accessed=4 * NB * NB * 4, transcendentals=0)


def factor_first(first, second):
    return pl.pallas_call(
        functools.partial(factor_first_kernel, COUNT - 1),
        out_shape=(SQUARE, SQUARE),
        in_specs=[IN_VMEM] * 2,
        out_specs=(IN_VMEM,) * 2,
        compiler_params=PARAMS,
        cost_estimate=FACTOR_COST,
        name="factor_first",
    )(first, second)


def factor_last(work, inv_t):
    return pl.pallas_call(
        functools.partial(factor_last_kernel, COUNT - 1),
        out_shape=(SQUARE, SQUARE, SQUARE),
        in_specs=[IN_VMEM] * 2,
        out_specs=(IN_VMEM,) * 3,
        compiler_params=PARAMS,
        cost_estimate=FACTOR_COST,
        name="factor_last",
    )(work, inv_t)


def update_kernel(spans, ahead, offset, tile, source_count, info, *refs):
    count = spans[-1][0] + 1
    inv_t_ref, matrix_ref = refs[:2]
    begin = 2 + len(spans)
    chunks = refs[2:begin]
    sources = refs[begin : begin + source_count]
    if ahead:
        factor_ref, inv_ref = refs[begin + source_count : begin + source_count + 2]
    out_ref = refs[-12 - ahead]
    across, rows, arrived, panel, panel3, left, right = refs[-11:-4]
    chunk_sems, row_sems, across_sem, out_sem = refs[-4:]
    i, j = pl.program_id(0), pl.program_id(1)
    tiles = across.shape[1] // tile
    half, deep = NB // 2, DEPTH // 2
    first_row = jnp.logical_and(info[0] == 0, info[2 + offset + jnp.maximum(i - ahead, 0)] == 0)
    first_col = jnp.logical_and(info[1] == 0, j == 0)

    def chunk_copy(k):
        n, first, size = spans[k]
        return pltpu.make_async_copy(chunks[k], arrived.at[n, pl.ds(first, size)], chunk_sems.at[k])

    def row_copy(n, t):
        place = pl.ds(t * tile, tile)
        return pltpu.make_async_copy(
            sources[n].at[pl.ds(0, NB), place], rows.at[:, place], row_sems.at[t]
        )

    @pl.when(jnp.logical_and(i == 0, j == 0))
    def _():
        if ahead:
            for n in range(source_count):

                @pl.when(info[0] == n)
                def _():
                    for t in range(tiles):
                        row_copy(n, t).start()

        for k in range(len(spans)):
            chunk_copy(k).start()
        if ahead:
            store_parts(left, inv_ref[...], 1, LEFT_PARTS)
        else:
            pltpu.make_async_copy(sources[0], across, across_sem).start()

    if ahead:

        @pl.when(i == 0)
        def _():
            for t in range(tiles):

                @pl.when(j == t)
                def _():
                    row_copy(0, t).wait()
                    for c in range(t * tile, (t + 1) * tile, NB):
                        store_parts(right, rows[:, c : c + NB], 0, RIGHT_PARTS)
                        for h in range(2):
                            part = slice(h * half, (h + 1) * half)
                            value = jnp.dot(
                                left[part, : (h + 1) * deep],
                                right[: (h + 1) * deep],
                                preferred_element_type=jnp.float32,
                            )
                            high, low = split2(value)
                            across[h * half : (h + 1) * half, c : c + NB] = high
                            across[NB + h * half : NB + (h + 1) * half, c : c + NB] = high
                            across[2 * NB + h * half : 2 * NB + (h + 1) * half, c : c + NB] = low

        handed = pltpu.make_async_copy(across, refs[-12], out_sem)

        @pl.when(jnp.logical_and(i == 1, j == 0))
        def _():
            handed.start()

        @pl.when(jnp.logical_and(i == count, j == tiles - 1))
        def _():
            handed.wait()

    @pl.when(jnp.logical_and(i == ahead, j == 0))
    def _():
        store_parts(right, inv_t_ref[...], 0, RIGHT_PARTS)

    @pl.when(jnp.logical_and(i >= ahead, j == 0))
    def _():
        for n in range(count):

            @pl.when(i == n + ahead)
            def _():
                for k in range(len(spans)):
                    if spans[k][0] == n:
                        chunk_copy(k).wait()
                store_parts(left, arrived[n], 1, LEFT_PARTS)

        for h in range(2):
            part = slice(h * half, (h + 1) * half)
            value = jnp.dot(
                left[:, : (h + 1) * deep],
                right[: (h + 1) * deep, part],
                preferred_element_type=jnp.float32,
            )
            panel[:, part] = value
            high, low = split2(value)
            panel3[:, h * half : (h + 1) * half] = high
            panel3[:, NB + h * half : NB + (h + 1) * half] = low
            panel3[:, 2 * NB + h * half : 2 * NB + (h + 1) * half] = high

        if ahead:

            @pl.when(first_row)
            def _():
                panel[...] = factor_ref[...]

    if not ahead:

        @pl.when(jnp.logical_and(i == 0, j == 0))
        def _():
            pltpu.make_async_copy(sources[0], across, across_sem).wait()

    @pl.when(jnp.logical_and(i >= ahead, first_row))
    def _():
        out_ref[...] = jnp.zeros_like(out_ref)

    @pl.when(jnp.logical_and(i >= ahead, jnp.logical_not(first_row)))
    def _():
        columns = pl.ds(pl.multiple_of(j * tile, tile), tile)
        product = jnp.dot(panel3[...], across[:, columns], preferred_element_type=jnp.float32)
        out_ref[...] = matrix_ref[...] - product

    @pl.when(jnp.logical_and(i >= ahead, first_col))
    def _():
        out_ref[:, :NB] = panel[...]


def update(info, offset, chunks, factor, inv, inv_t, matrix, sources, base):
    count = len(chunks)
    pieces, spans = [], []
    for n, chunk in enumerate(chunks):
        first = 0
        for piece in chunk if isinstance(chunk, tuple) else (chunk,):
            pieces.append(piece)
            spans.append((n, first, piece.shape[0]))
            first += piece.shape[0]
    ahead = 1 if base is None else 0
    width = matrix.shape[1]
    tile = 2 * NB if width % (2 * NB) == 0 else NB
    whole = lambda i, j, info: (0, 0)

    def moving(i, j, info):
        n = i - ahead
        return info[2 + offset + jnp.maximum(n, 0)], jnp.where(n < 0, 0, j)

    square = pl.BlockSpec((NB, NB), whole)
    block = pl.BlockSpec((NB, tile), moving)
    across = jax.ShapeDtypeStruct((3 * NB, width), jnp.bfloat16)
    in_specs = [square, block] + [ANYWHERE] * (len(pieces) + len(sources))
    operands = [info, inv_t, matrix, *pieces, *sources]
    out_shape, out_specs, aliases = [jax.ShapeDtypeStruct(matrix.shape, jnp.float32)], [block], {}
    if ahead:
        in_specs += [square] * 2
        operands += [factor, inv]
        out_shape.append(across)
        out_specs.append(ANYWHERE)
    else:
        in_specs.append(ANYWHERE)
        operands.append(base)
        aliases = {len(operands) - 1: 0}
    return pl.pallas_call(
        functools.partial(update_kernel, spans, ahead, offset, tile, len(sources)),
        grid_spec=pltpu.PrefetchScalarGridSpec(
            num_scalar_prefetch=1,
            grid=(count + ahead, width // tile),
            in_specs=in_specs,
            out_specs=out_specs,
            scratch_shapes=[
                pltpu.VMEM(across.shape, jnp.bfloat16),
                pltpu.VMEM((NB, width) if ahead else (8, 128), jnp.float32),
                pltpu.VMEM((count, NB, NB), jnp.float32),
                pltpu.VMEM((NB, NB), jnp.float32),
                pltpu.VMEM((NB, 3 * NB), jnp.bfloat16),
                pltpu.VMEM((NB, DEPTH), jnp.bfloat16),
                pltpu.VMEM((DEPTH, NB), jnp.bfloat16),
                pltpu.SemaphoreType.DMA((len(pieces),)),
                pltpu.SemaphoreType.DMA((width // tile,)),
                pltpu.SemaphoreType.DMA,
                pltpu.SemaphoreType.DMA,
            ],
        ),
        out_shape=out_shape,
        input_output_aliases=aliases,
        compiler_params=PARAMS,
        cost_estimate=pl.CostEstimate(
            flops=6 * (count + ahead) * NB * NB * (width + 2 * NB),
            bytes_accessed=8 * count * NB * width,
            transcendentals=0,
        ),
        name="update_rows",
    )(*operands)


def tree_stages(order):
    reached, done, stages = [0], 0, []
    for bit in order:
        stages.append(([(n, n | bit) for n in reached], bit, done))
        reached = reached + [n | bit for n in reached]
        done |= bit
    return stages


def bits_of(size):
    return [1 << n for n in range(size.bit_length() - 1)]


def corner_orders(rows_axis, cols_axis):
    low = bits_of(cols_axis)
    high = [cols_axis * bit for bit in bits_of(rows_axis)]
    core, across = high[:1], high[:0:-1]
    near, far = low[:1], low[:0:-1]
    return across + near + far + core, across + far + near + core


def spread_apart(held, axis, bit):
    return held + [(n | bit, lax.ppermute(v, axis, [(n, n | bit)])) for n, v in held]


def ring_positions(cols_axis):
    half = cols_axis // 2
    return [2 * n for n in range(half)] + [2 * n + 1 for n in reversed(range(half))]


def scatter_pairs(t, rows_axis, cols_axis):
    pairs = []
    for r in range(cols_axis):
        h, target = divmod(r, rows_axis)
        pairs.append((r, target * cols_axis + h * rows_axis + (target ^ t)))
    return [(a, b) for a, b in pairs if a != b]


def ring_shifts(cols_axis):
    shifts = [0]
    last = cols_axis // 2 - 1
    for step in range(1, last):
        shifts += [-step, step]
    return shifts + [-last, last, cols_axis // 2]


def place_table(rows_axis, cols_axis, balanced, row_blocks):
    ring = ring_positions(cols_axis)
    groups = cols_axis // rows_axis
    table = []
    for p in range(rows_axis):
        for q in range(cols_axis):
            if balanced:
                places = []
                for shift in ring_shifts(cols_axis):
                    source = ring[(ring.index(q) + shift) % cols_axis]
                    places.append(groups * ((source % rows_axis) ^ p) + source // rows_axis)
            else:
                places = list(range(row_blocks))
            table.append([p, q] + places)
    return np.array(table, np.int32)


def from_root(value, axis, source):
    kept = jnp.where(lax.axis_index(axis) == source, value, 0).astype(value.dtype)
    return lax.psum(kept, axis)


def tie(*values):
    return lax.optimization_barrier(values)


def on_device(matrix):
    rows_axis = lax.axis_size("row")
    cols_axis = lax.axis_size("col")
    both = ("row", "col")
    index = lax.axis_index("row") * cols_axis + lax.axis_index("col")
    row_blocks = matrix.shape[0] // NB
    col_blocks = matrix.shape[1] // NB
    balanced = row_blocks == cols_axis and col_blocks == rows_axis
    table = jnp.asarray(place_table(rows_axis, cols_axis, balanced, row_blocks))
    places = lax.dynamic_slice_in_dim(table, index, 1, 0)[0]

    parts = list(pack_corner(matrix))
    stages = [tree_stages(order) for order in corner_orders(rows_axis, cols_axis)]
    *blocks, head = turn_blocks(matrix, col_blocks)
    first_bit, *other_bits = bits_of(rows_axis)[::-1]
    far = None
    for step in range(len(stages[0])):
        if step == len(stages[0]) - 1 and balanced and False:
            parts[0], parts[1], far = tie(*parts, far)
        came = [lax.ppermute(parts[n], both, stages[n][step][0]) for n in range(2)]
        for n in range(2):
            _, bit, done = stages[n][step]
            parts[n] = jnp.where((index & ~done) == bit, came[n], parts[n])
        if step == 0:
            parts[0], parts[1], head, *blocks = tie(*parts, head, *blocks)
        if step == 0 and balanced:
            _, far = spread_apart([(0, head)], "row", first_bit)[1]
        if step == len(stages[0]) - 2 and balanced:
            parts[0], parts[1], *blocks = tie(*parts, *blocks)
            pieces = [
                lax.ppermute(blocks[t], both, scatter_pairs(t, rows_axis, cols_axis))
                for t in reversed(range(col_blocks))
            ]

    if balanced:
        ring = ring_positions(cols_axis)
        up = [(ring[n], ring[(n + 1) % cols_axis]) for n in range(cols_axis)]
        down = [(b, a) for a, b in up]

        def advance(going, coming):
            return lax.ppermute(going, "col", up), lax.ppermute(coming, "col", down)

        own = [(0, head)]
        for bit in other_bits:
            own = spread_apart(own, "row", bit)
        work, inv_t = factor_first(*parts)
        work, far, *pieces = tie(work, far, *pieces)
        far = [(first_bit, far)]
        for bit in other_bits:
            far = spread_apart(far, "row", bit)
        held = own + far
        own_block = jnp.logical_and(index < cols_axis, index % rows_axis == 0)
        chunk = jnp.where(own_block, blocks[0], functools.reduce(jnp.add, pieces))
        chunks = [[chunk]]
        going, coming = advance(chunk, chunk)
        work, chunk = tie(work, chunk)
        factor, inv, inv_t = factor_last(work, inv_t)
    else:
        column = from_root(matrix[:, :NB], "col", 0)
        chunks = [[column[s * NB : (s + 1) * NB] for s in range(row_blocks)]]
        factor, inv, inv_t = factor_last(*factor_first(*parts))
        held = [(0, head)]
        for bit in [first_bit, *other_bits]:
            held = spread_apart(held, "row", bit)

    sources = [matrix] + [v for _, v in sorted(held, key=lambda entry: entry[0])][1:]
    place = len(chunks[0])
    out, across = update(places, 0, chunks[0], factor, inv, inv_t, matrix, sources, None)

    def more(out, part, place):
        return update(places, place, part, factor, inv, inv_t, matrix, [across], out)[0]

    if balanced:
        for step in range(1, cols_axis // 2):
            out, going, coming = tie(out, going, coming)
            part = [going, coming]
            if step < cols_axis // 2 - 1:
                going, coming = advance(going, coming)
            else:
                top = lax.ppermute(going[: NB // 2], "col", up)
                bottom = lax.ppermute(coming[NB // 2 :], "col", down)
            out = more(out, part, place)
            place += len(part)
        out = more(out, [(top, bottom)], place)
    return out


def solution(mesh):
    in_specs = (P("row", "col"),)
    out_specs = P("row", "col")
    return jax.shard_map(
        on_device, mesh=mesh, in_specs=in_specs, out_specs=out_specs, check_vma=False
    )
```
